256 devices in a mesh: sta: 64 (over z, y, core), win: 4 (over x).
Axes of the slice: x: 4, y: 4, z: 8, core: 2. Of those that a mesh axis runs over, the one named last changes fastest.
Arguments:
- spectra: float32 [4, 1024, 8192], P('win', 'sta')
- wanted: int32 [64, 64, 3], P('sta'), may hold values from 0 to 15, as said below
- pairs: int32 [16384, 2], P('sta'), may hold values from 0 to 191, as said below
- counts: int32 [64], P('sta'), may hold values from 32 to 256, as said below
Outputs:
- correlations: float32 [16384, 1024], P(('sta', 'win'))
The draws below stay inside these ranges and needn't reach their ends.
Inputs may be any that keep to these rules, and one draw needn't show every extreme that they name: `wanted`: each source's 3 entries for one owner are distinct local stations. `pairs`: the two entries of a pair slot differ. `counts`: some owner has all 256 slots live in every draw.
All inputs are finite; a program needn't handle non-finite values.
Results may differ from the reference program's by a relative error of at most 0.0043.
Values may be sent and summed in bfloat16 or wider, within the bound.
A program may use at most 128 MiB of HBM per device.

```python
import math
import jax
import jax.numpy as jnp
from jax import lax

F = 4096
BAND = 64
LAGS = 1024
FREQ_BLOCK = 512
CAP = 3
S_DEV = 16
PAIR_DEV = 256
STATIONS = 1024
WINDOWS = 4
PAIRS = 16384
RECV = 192
N_STA = 64


def draw_spectra(key, part):
    key = jax.random.fold_in(key, 11)
    key_vals, key_scale = jax.random.split(key)
    bands = F // BAND
    values = jax.random.normal(key_vals, (WINDOWS, STATIONS, 2, bands, BAND), jnp.float32)
    scales = jnp.exp(jax.random.uniform(key_scale, (WINDOWS, STATIONS, 1, bands, 1), jnp.float32, 0.0, math.log(10.0)))
    return (values * scales).reshape(WINDOWS, STATIONS, 2 * F)


def draw_wanted(key, part):
    key = jax.random.fold_in(key, 12)
    scores = jax.random.randint(key, (N_STA, N_STA, S_DEV), 0, 1 << 20) * S_DEV + jnp.arange(S_DEV, dtype=jnp.int32)
    order = jnp.argsort(scores, axis=-1, stable=True)
    return order[..., :CAP].astype(jnp.int32)


def draw_pairs(key, part):
    key = jax.random.fold_in(key, 13)
    key_first, key_gap = jax.random.split(key)
    first = jax.random.randint(key_first, (PAIRS,), 0, RECV)
    gap = jax.random.randint(key_gap, (PAIRS,), 1, RECV)
    second = jnp.mod(first + gap, RECV)
    return jnp.stack([first, second], axis=1).astype(jnp.int32)


def draw_counts(key, part):
    key = jax.random.fold_in(key, 14)
    key_count, key_full = jax.random.split(key)
    lowest = max(PAIR_DEV // 8, 1)
    values = jax.random.randint(key_count, (N_STA,), lowest, PAIR_DEV // 3 + 1)
    busiest = jax.random.randint(key_full, (), 0, N_STA)
    return values.at[busiest].set(PAIR_DEV).astype(jnp.int32)


def setup_inputs(seed: int = 0) -> dict:
    key_list = jax.random.split(jax.random.key(seed), 5)
    return {
        "spectra": draw_spectra(jax.random.fold_in(key_list[4], 71), 0),
        "wanted": draw_wanted(jax.random.fold_in(key_list[4], 71), 0),
        "pairs": draw_pairs(jax.random.fold_in(key_list[4], 71), 0),
        "counts": draw_counts(jax.random.fold_in(key_list[4], 71), 0),
    }


def whiten(spectra):
    width = spectra.shape[-1] // 2
    real_part = spectra[..., :width]
    imag_part = spectra[..., width:]
    magnitude = jnp.sqrt(real_part * real_part + imag_part * imag_part)
    shape = magnitude.shape[:-1] + (width // BAND, BAND)
    band = lax.optimization_barrier(jnp.mean(magnitude.reshape(shape), axis=-1)) + 1e-06
    band = jnp.repeat(band, BAND, axis=-1)
    scale = jnp.concatenate([band, band], axis=-1)
    return (spectra / scale).astype(jnp.bfloat16)

def cross_of(left, right):
    width = left.shape[-1] // 2
    left = left.astype(jnp.float32)
    right = right.astype(jnp.float32)
    lre, lim = (left[..., :width], left[..., width:])
    rre, rim = (right[..., :width], right[..., width:])
    return jnp.concatenate([lre * rre + lim * rim, lre * rim - lim * rre], axis=-1)

def inverse(stack):
    width = stack.shape[1] // 2
    real_part = stack[:, :width]
    imag_part = stack[:, width:]
    lag_index = jnp.arange(LAGS, dtype=jnp.int32) - LAGS // 2
    period = 2 * width

    def step(block, total):
        start = (block * FREQ_BLOCK).astype(jnp.int32)
        freq = start + jnp.arange(FREQ_BLOCK, dtype=jnp.int32)
        phase = jnp.mod(freq[:, None] * lag_index[None, :], period)
        angle = phase.astype(jnp.float32) * (2.0 * math.pi / period)
        re_block = lax.dynamic_slice_in_dim(real_part, start, FREQ_BLOCK, 1)
        im_block = lax.dynamic_slice_in_dim(imag_part, start, FREQ_BLOCK, 1)
        total = total + jnp.dot(re_block, jnp.cos(angle), precision=lax.Precision.HIGHEST, preferred_element_type=jnp.float32)
        total = total - jnp.dot(im_block, jnp.sin(angle), precision=lax.Precision.HIGHEST, preferred_element_type=jnp.float32)
        return total
    zeros = jnp.zeros((stack.shape[0], LAGS), jnp.float32)
    total = lax.fori_loop(0, width // FREQ_BLOCK, step, zeros)
    return total / math.sqrt(width)

def reference(spectra, wanted, pairs, counts):
    white = whiten(spectra)

    def one_owner(owner):
        slots = lax.dynamic_slice_in_dim(pairs, (owner * PAIR_DEV).astype(jnp.int32), PAIR_DEV, 0)
        source_a = slots[:, 0] // CAP
        source_b = slots[:, 1] // CAP
        station_a = source_a * S_DEV + wanted[source_a, owner, slots[:, 0] % CAP]
        station_b = source_b * S_DEV + wanted[source_b, owner, slots[:, 1] % CAP]
        left = jnp.take(white, station_a, axis=1)
        right = jnp.take(white, station_b, axis=1)
        stack = lax.optimization_barrier(jnp.sum(cross_of(left, right), axis=0))
        corr = inverse(stack)
        live = jnp.arange(PAIR_DEV, dtype=jnp.int32) < counts[owner]
        return jnp.where(live[:, None], corr, jnp.zeros_like(corr))
    result = lax.map(one_owner, jnp.arange(N_STA, dtype=jnp.int32))
    return result.reshape(PAIRS, LAGS)
```

```python
import math

import jax
import jax.numpy as jnp
import numpy as np
from jax import lax
from jax.sharding import PartitionSpec as P

BAND = 64
LAGS = 1024


def whiten(spectra):
    width = spectra.shape[-1] // 2
    real_part = spectra[..., :width]
    imag_part = spectra[..., width:]
    magnitude = jnp.sqrt(real_part * real_part + imag_part * imag_part)
    shape = magnitude.shape[:-1] + (width // BAND, BAND)
    band = jnp.mean(magnitude.reshape(shape), axis=-1) + 1e-06
    band = jnp.repeat(band, BAND, axis=-1)
    scale = jnp.concatenate([band, band], axis=-1)
    return (spectra / scale).astype(jnp.bfloat16)


def tables(width, parts):
    quarter = width // parts
    fine = 32
    lag = np.arange(LAGS, dtype=np.int64) - LAGS // 2
    period = 2 * width

    def both(freq):
        angle = (freq[:, None] * lag[None, :]) % period * (2.0 * np.pi / period)
        return np.stack([np.cos(angle), np.sin(angle)]).astype(np.float32)

    return both(np.arange(fine)), both(np.arange(0, width, fine)).reshape(2, parts, quarter // fine, LAGS)


def local(spectra, wanted, pairs, counts):
    white = whiten(spectra)[0]
    owners = wanted.shape[1]
    per_owner = wanted.shape[2]
    width = white.shape[1] // 2
    parts = lax.axis_size("win")
    me = lax.axis_index("win")
    quarter = width // parts
    stations = white.shape[0]
    split = white.reshape(stations, 2, parts, quarter)
    split = jnp.transpose(split, (2, 0, 1, 3))
    split = lax.all_to_all(split, "win", split_axis=0, concat_axis=0, tiled=True)
    mixed = jnp.transpose(split, (1, 0, 2, 3)).reshape(stations, parts * 2 * quarter)
    outgoing = jnp.take(mixed, wanted[0].reshape(-1), axis=0)
    received = lax.all_to_all(outgoing, "sta", split_axis=0, concat_axis=0, tiled=True)
    left = jnp.take(received, pairs[:, 0], axis=0).reshape(-1, parts, 2, quarter).astype(jnp.float32)
    right = jnp.take(received, pairs[:, 1], axis=0).reshape(-1, parts, 2, quarter).astype(jnp.float32)
    lre, lim = left[:, :, 0], left[:, :, 1]
    rre, rim = right[:, :, 0], right[:, :, 1]
    stack_re = jnp.sum(lre * rre + lim * rim, axis=1)
    stack_im = jnp.sum(lre * rim - lim * rre, axis=1)
    fine, coarse = tables(width, parts)
    mine = lax.dynamic_index_in_dim(jnp.asarray(coarse), me, 1, keepdims=False)
    cc, sc = mine[0][:, None], mine[1][:, None]
    cf, sf = fine[0][None], fine[1][None]
    cos = (cc * cf - sc * sf).reshape(quarter, LAGS)
    sin = (sc * cf + cc * sf).reshape(quarter, LAGS)
    stack = jnp.concatenate([stack_re, stack_im], axis=1)
    wave = jnp.concatenate([cos, -sin], axis=0)
    partial = jnp.dot(stack, wave, precision=lax.Precision.HIGHEST, preferred_element_type=jnp.float32)
    corr = lax.psum_scatter(partial, "win", scatter_dimension=0, tiled=True) / math.sqrt(width)
    share = corr.shape[0]
    position = me * share + jnp.arange(share, dtype=jnp.int32)
    live = position < counts[0]
    return jnp.where(live[:, None], corr, jnp.zeros_like(corr))


def solution(mesh):
    placed = (P("win", "sta", None), P("sta", None, None), P("sta", None), P("sta"))
    return jax.shard_map(
        local, mesh=mesh, in_specs=placed, out_specs=P(("sta", "win"), None), check_vma=False
    )
```

```python
import functools
import math

import jax
import jax.numpy as jnp
import numpy as np
from jax import lax
from jax.experimental import pallas as pl
from jax.experimental.pallas import tpu as pltpu
from jax.sharding import PartitionSpec as P

BAND = 64
LAGS = 1024
FINE = 32
NZ, NY, NC, NX = 8, 4, 2, 4
YC = NY * NC
STATIONS = 16
CAP = 3
WIDTH = 4096
QUARTER = WIDTH // NX
ROWS = QUARTER // 128
SLOTS = 256
SHARE = SLOTS // NX
RECV = NZ * YC * CAP
LAG_STEP = 256
SHIFT = (0, 1, 3, 2)
MESH = pl.DeviceIdType.MESH


def tables():
    lag = np.arange(LAGS, dtype=np.int64) - LAGS // 2
    period = 2 * WIDTH

    def both(freq):
        angle = (freq[:, None] * lag[None, :]) % period * (2.0 * np.pi / period)
        return np.stack([np.cos(angle), np.sin(angle)]).astype(np.float32)

    return both(np.arange(FINE)), both(np.arange(0, WIDTH, FINE))


def kernel(
    spectra, table, pairs, counts, fine_hbm, coarse_hbm, out,
    white32, quarters, held, work, stage, landed, wide, stack, lhs, wave, total, parts_out, parts_in,
    table_all, table_smem, fine, coarse,
    x_send, x_recv, z_send, z_recv, t_send, t_recv, y_send, y_recv, r_send, r_recv, local_sem, smem_sem,
):
    win = lax.axis_index("win")
    sta = lax.axis_index("sta")
    z = sta // YC
    yc = lax.rem(sta, YC)

    def at_x(step):
        return (sta, lax.rem(win + step, NX))

    def at_z(step):
        return (lax.rem(z + step + NZ, NZ) * YC + yc, win)

    def at_yc(step):
        return (z * YC + lax.rem(yc + step, YC), win)

    barrier = pltpu.get_barrier_semaphore()
    for step in (1, 2, 3):
        pl.semaphore_signal(barrier, inc=1, device_id=at_x(step), device_id_type=MESH)
    for step in (1, -1):
        pl.semaphore_signal(barrier, inc=1, device_id=at_z(step), device_id_type=MESH)
    for step in range(1, YC):
        pl.semaphore_signal(barrier, inc=1, device_id=at_yc(step), device_id_type=MESH)

    load_fine = pltpu.make_async_copy(fine_hbm, fine, local_sem.at[0])
    load_fine.start()
    own_coarse = coarse_hbm.at[:, pl.ds(pl.multiple_of(win * FINE, FINE), FINE)]
    load_coarse = pltpu.make_async_copy(own_coarse, coarse, local_sem.at[1])
    load_coarse.start()
    table_all[z] = table[...]

    lane_r = lax.broadcasted_iota(jnp.int32, (128, 128), 0) // BAND
    lane_c = lax.broadcasted_iota(jnp.int32, (128, 128), 1) // BAND
    same = jnp.where(lane_r == lane_c, 1.0, 0.0).astype(jnp.float32)
    chunks = WIDTH // 128

    @pl.loop(0, chunks // 4)
    def _(group):
        for part in range(4):
            j = group * 4 + part
            re = spectra[:, pl.ds(pl.multiple_of(j * 128, 128), 128)]
            im = spectra[:, pl.ds(pl.multiple_of(WIDTH + j * 128, 128), 128)]
            mag = jnp.sqrt(re * re + im * im)
            sums = jnp.dot(mag, same, precision=lax.Precision.HIGHEST, preferred_element_type=jnp.float32)
            band = sums * (1.0 / BAND) + 1e-06
            white32[pl.ds(j, STATIONS, stride=2 * chunks), :] = re / band
            white32[pl.ds(chunks + j, STATIONS, stride=2 * chunks), :] = im / band

    @pl.loop(0, STATIONS)
    def _(s):
        for step in range(NX):
            quarter = lax.rem(win + step, NX)
            base = s * 2 * chunks + quarter * ROWS
            re = white32[pl.ds(pl.multiple_of(base, ROWS), ROWS), :]
            im = white32[pl.ds(pl.multiple_of(base + chunks, ROWS), ROWS), :]
            slab = jnp.concatenate([re, im], axis=0).astype(jnp.bfloat16)
            if step == 0:
                held[0, z, s] = slab
            else:
                quarters[step - 1, s] = slab

    pl.semaphore_wait(barrier, 3 + 2 + YC - 1)

    def x_copy(step):
        place = SHIFT.index((NX - step) % NX)
        return pltpu.make_async_remote_copy(
            src_ref=quarters.at[step - 1], dst_ref=held.at[place, z],
            send_sem=x_send.at[place - 1], recv_sem=x_recv.at[place - 1],
            device_id=at_x(step), device_id_type=MESH,
        )

    def z_copy(i, way, k):
        source = lax.rem(z - way * k + NZ, NZ)
        ref = held.at[i, source]
        if k == NZ // 2 - 1:
            ref = ref.at[pl.ds(0 if way == 1 else STATIONS // 2, STATIONS // 2)]
        side = 0 if way == 1 else 1
        return pltpu.make_async_remote_copy(
            src_ref=ref, dst_ref=ref, send_sem=z_send.at[i, side, k], recv_sem=z_recv.at[i, side, k],
            device_id=at_z(way), device_id_type=MESH,
        )

    def z_wait(i, way, k):
        source = lax.rem(z - way * k + NZ, NZ)
        ref = held.at[i, source]
        if k == NZ // 2:
            ref = ref.at[pl.ds(0 if way == 1 else STATIONS // 2, STATIONS // 2)]
        side = 0 if way == 1 else 1
        pltpu.make_async_copy(ref, ref, z_recv.at[i, side, k - 1]).wait()

    def t_copy(way, k):
        source = lax.rem(z - way * k + NZ, NZ)
        side = 0 if way == 1 else 1
        return pltpu.make_async_remote_copy(
            src_ref=table_all.at[source], dst_ref=table_all.at[source],
            send_sem=t_send.at[side, k], recv_sem=t_recv.at[side, k],
            device_id=at_z(way), device_id_type=MESH,
        )

    def t_wait(way, k):
        source = lax.rem(z - way * k + NZ, NZ)
        side = 0 if way == 1 else 1
        pltpu.make_async_copy(table_all.at[source], table_all.at[source], t_recv.at[side, k - 1]).wait()

    def to_smem(source):
        copy = pltpu.make_async_copy(table_all.at[source], table_smem.at[source], smem_sem)
        copy.start()
        copy.wait()

    def pick(i, source):
        for s in range(STATIONS):
            work[s] = held[i, source, s]
        place = source * YC + yc

        @pl.loop(0, YC)
        def _(step):
            to = lax.rem(yc + step, YC)
            for c in range(CAP):
                wanted = table_smem[source, z, to * CAP + c]
                stage[i, source, step, c] = work[wanted]

            @pl.when(step > 0)
            def _():
                pltpu.make_async_remote_copy(
                    src_ref=stage.at[i, source, step], dst_ref=landed.at[i, pl.ds(place * CAP, CAP)],
                    send_sem=y_send.at[i], recv_sem=y_recv.at[i],
                    device_id=at_yc(step), device_id_type=MESH,
                ).start()

        for c in range(CAP):
            landed[i, place * CAP + c] = stage[i, source, 0, c]

    half = NZ // 2
    for way in (1, -1):
        z_copy(0, way, 0).start()
        t_copy(way, 0).start()
    for step in (1, 3, 2):
        x_copy(step).start()
    to_smem(z)

    for t in range(NX + half):
        for i in range(NX):
            k = t - i
            if k < 0 or k > half:
                continue
            if k == 0:
                if i > 0:
                    pltpu.make_async_copy(quarters.at[0], held.at[i, z], x_recv.at[i - 1]).wait()
                    for way in (1, -1):
                        z_copy(i, way, 0).start()
            else:
                for way in (1, -1):
                    z_wait(i, way, k)
                    if k < half:
                        z_copy(i, way, k).start()
                if i == 0:
                    t_wait(1, k)
                    if k < half:
                        t_copy(1, k).start()
                        t_wait(-1, k)
                        if k < half - 1:
                            t_copy(-1, k).start()
        for i in range(NX):
            k = t - i
            if k < 0 or k > half:
                continue
            sources = [lax.rem(z - k + NZ, NZ)]
            if 0 < k < half:
                sources.append(lax.rem(z + k, NZ))
            for source in sources:
                if i == 0 and k > 0:
                    to_smem(source)
                pick(i, source)

    load_fine.wait()
    load_coarse.wait()

    @pl.loop(0, QUARTER // FINE)
    def _(j):
        cc = coarse[0, pl.ds(j, 1), :]
        sc = coarse[1, pl.ds(j, 1), :]
        rows = pl.ds(pl.multiple_of(j * FINE, FINE), FINE)
        later = pl.ds(pl.multiple_of(QUARTER + j * FINE, FINE), FINE)
        wave[rows, :] = (cc * fine[0] - sc * fine[1]).astype(jnp.bfloat16)
        wave[later, :] = (-(sc * fine[0] + cc * fine[1])).astype(jnp.bfloat16)

    sent = (RECV // YC) * (YC - 1)
    for i in range(NX):
        block = landed.at[i, pl.ds(0, sent)]
        pltpu.make_async_copy(block, block, y_recv.at[i]).wait()

        @pl.loop(0, RECV // 8)
        def _(g):
            for e in range(8):
                wide[g * 8 + e] = landed[i, g * 8 + e].astype(jnp.float32)

        @pl.loop(0, SLOTS // 8)
        def _(g):
            for e in range(8):
                p = g * 8 + e
                left = wide[pairs[p, 0]]
                right = wide[pairs[p, 1]]
                lre, lim = left[:ROWS], left[ROWS:]
                rre, rim = right[:ROWS], right[ROWS:]
                re = lre * rre + lim * rim
                im = lre * rim - lim * rre
                first = pl.ds(pl.multiple_of(p * 2 * ROWS, ROWS), ROWS)
                second = pl.ds(pl.multiple_of(p * 2 * ROWS + ROWS, ROWS), ROWS)
                if i == 0:
                    stack[first, :] = re
                    stack[second, :] = im
                else:
                    stack[first, :] += re
                    stack[second, :] += im

    for j in range(2 * ROWS):
        lhs[:, j * 128 : (j + 1) * 128] = stack[pl.ds(j, SLOTS, stride=2 * ROWS), :].astype(jnp.bfloat16)

    def r_copy(step, n):
        return pltpu.make_async_remote_copy(
            src_ref=parts_out.at[step - 1, n], dst_ref=parts_in.at[step - 1, n],
            send_sem=r_send.at[step - 1, n], recv_sem=r_recv.at[step - 1, n],
            device_id=at_x(step), device_id_type=MESH,
        )

    steps = LAGS // LAG_STEP
    for n in range(steps):
        columns = slice(n * LAG_STEP, (n + 1) * LAG_STEP)
        total[n] = jnp.dot(lhs[...], wave[:, columns], preferred_element_type=jnp.float32)
        for step in (2, 1, 3):
            rows = pl.ds(pl.multiple_of(lax.rem(win + step, NX) * SHARE, SHARE), SHARE)
            parts_out[step - 1, n] = total[n, rows, :].astype(jnp.bfloat16)
            r_copy(step, n).start()

    rows = pl.ds(pl.multiple_of(win * SHARE, SHARE), SHARE)
    live = win * SHARE + lax.broadcasted_iota(jnp.int32, (SHARE, LAG_STEP), 0) < counts[0]
    for n in range(steps):
        value = total[n, rows, :]
        for step in (1, 3, 2):
            r_copy(step, n).wait_recv()
            value = value + parts_in[step - 1, n].astype(jnp.float32)
        value = value * (1.0 / math.sqrt(WIDTH))
        out[:, n * LAG_STEP : (n + 1) * LAG_STEP] = jnp.where(live, value, 0.0)

    for step in (1, 2, 3):
        x_copy(step).wait_send()
        for n in range(steps):
            r_copy(step, n).wait_send()
    for i in range(NX):
        block = landed.at[i, pl.ds(0, sent)]
        pltpu.make_async_copy(block, block, y_send.at[i]).wait()
        for way in (1, -1):
            for k in range(half):
                z_copy(i, way, k).wait_send()
    for k in range(half):
        t_copy(1, k).wait_send()
        if k < half - 1:
            t_copy(-1, k).wait_send()


def local(spectra, wanted, pairs, counts):
    table = jnp.pad(wanted.reshape(NZ, YC * CAP), ((0, 0), (0, 128 - YC * CAP)))
    fine, coarse = tables()
    vmem = pl.BlockSpec(memory_space=pltpu.VMEM)
    smem = pl.BlockSpec(memory_space=pltpu.SMEM)
    anywhere = pl.BlockSpec(memory_space=pl.ANY)
    half = NZ // 2
    steps = LAGS // LAG_STEP
    bf16, f32 = jnp.bfloat16, jnp.float32
    dma = pltpu.SemaphoreType.DMA
    return pl.pallas_call(
        kernel,
        out_shape=jax.ShapeDtypeStruct((SHARE, LAGS), f32),
        in_specs=[vmem, vmem, smem, smem, anywhere, anywhere],
        out_specs=vmem,
        scratch_shapes=[
            pltpu.VMEM((STATIONS * 2 * (WIDTH // 128), 128), f32),
            pltpu.VMEM((NX - 1, STATIONS, 2 * ROWS, 128), bf16),
            pltpu.VMEM((NX, NZ, STATIONS, 2 * ROWS, 128), bf16),
            pltpu.VMEM((STATIONS, 2 * ROWS, 128), bf16),
            pltpu.VMEM((NX, NZ, YC, CAP, 2 * ROWS, 128), bf16),
            pltpu.VMEM((NX, RECV, 2 * ROWS, 128), bf16),
            pltpu.VMEM((RECV, 2 * ROWS, 128), f32),
            pltpu.VMEM((SLOTS * 2 * ROWS, 128), f32),
            pltpu.VMEM((SLOTS, 2 * QUARTER), bf16),
            pltpu.VMEM((2 * QUARTER, LAGS), bf16),
            pltpu.VMEM((steps, SLOTS, LAG_STEP), f32),
            pltpu.VMEM((NX - 1, steps, SHARE, LAG_STEP), bf16),
            pltpu.VMEM((NX - 1, steps, SHARE, LAG_STEP), bf16),
            pltpu.VMEM((NZ, 8, 128), jnp.int32),
            pltpu.SMEM((NZ, 8, 128), jnp.int32),
            pltpu.VMEM((2, FINE, LAGS), f32),
            pltpu.VMEM((2, QUARTER // FINE, LAGS), f32),
            dma((NX - 1,)), dma((NX - 1,)),
            dma((NX, 2, half)), dma((NX, 2, half)),
            dma((2, half)), dma((2, half)),
            dma((NX,)), dma((NX,)),
            dma((NX - 1, steps)), dma((NX - 1, steps)),
            dma((2,)), dma,
        ],
        compiler_params=pltpu.CompilerParams(
            collective_id=0, has_side_effects=True, vmem_limit_bytes=48 << 20
        ),
        name="correlate",
    )(spectra[0], table, pairs, counts, fine, coarse)


def solution(mesh):
    placed = (P("win", "sta", None), P("sta", None, None), P("sta", None), P("sta"))
    return jax.shard_map(
        local, mesh=mesh, in_specs=placed, out_specs=P(("sta", "win"), None), check_vma=False
    )
```

```python
import functools
import math

import jax
import jax.numpy as jnp
import numpy as np
from jax import lax
from jax.experimental import pallas as pl
from jax.experimental.pallas import tpu as pltpu
from jax.sharding import PartitionSpec as P

BAND = 64
LAGS = 1024
FINE = 32
NZ, NY, NC, NX = 8, 4, 2, 4
YC = NY * NC
STATIONS = 16
CAP = 3
WIDTH = 4096
QUARTER = WIDTH // NX
ROWS = QUARTER // 128
SLOTS = 256
SHARE = SLOTS // NX
RECV = NZ * YC * CAP
LAG_STEP = 256
SHIFT = (0, 1, 3, 2)
FAR = (0, 1)
REACH = 3
NEAR = 1 + 2 * REACH
ORDER = (
    "x0", "p00", "z01", "p01", "x1", "p10", "x2", "p20", "z02", "x3", "p30", "w0",
    "p02", "z11", "p11", "z21", "p21", "z31", "p31", "w1", "z03", "z12", "p03", "z22",
    "p22", "p12", "z04", "z32", "p04", "w2", "z13", "z23", "p13", "p23", "z33", "z14",
    "f0", "z24", "z34", "p14", "p24", "w3", "p33", "p32", "f1", "p34", "c0", "c2",
    "c1", "c3",
)
FIRST_FAR = [int(event[1]) for event in ORDER if event[0] == "f"][:1]
FIRST_CROSS = [int(event[1]) for event in ORDER if event[0] == "c"][:1]
WAVE_STEPS = 4
MESH = pl.DeviceIdType.MESH


def tables():
    lag = np.arange(LAGS, dtype=np.int64) - LAGS // 2
    period = 2 * WIDTH

    def both(freq):
        angle = (freq[:, None] * lag[None, :]) % period * (2.0 * np.pi / period)
        return np.stack([np.cos(angle), np.sin(angle)]).astype(np.float32)

    return both(np.arange(FINE)), both(np.arange(0, WIDTH, FINE))


def kernel(
    spectra_hbm, table_hbm, pairs_hbm, counts, fine_hbm, coarse_hbm, out,
    spectra, pairs, terms, sums, white32, quarters, held, work, stage, landed, wide, stack, lhs, wave, total, half_out, half_in, parts_out, parts_in,
    table_all, table_smem, fine, coarse,
    far, stage_far, table_far, table_far_smem, f_send, f_recv,
    x_send, x_recv, z_send, z_recv, t_send, t_recv, y_send, y_recv, h_send, h_recv, r_send, r_recv, local_sem, smem_sem,
):
    win = lax.axis_index("win")
    sta = lax.axis_index("sta")
    z = sta // YC
    yc = lax.rem(sta, YC)
    y = yc // NC
    core = lax.rem(yc, NC)
    across = lax.rem(y + NY // 2, NY) * NC + core

    def at_x(step):
        return (sta, lax.rem(win + step, NX))

    def at_z(step):
        return (lax.rem(z + step + NZ, NZ) * YC + yc, win)

    def at_yc(step):
        to = lax.rem(y + step // NC, NY) * NC + lax.rem(core + lax.rem(step, NC), NC)
        return to, (z * YC + to, win)

    def at_zc(step):
        along = step // NC
        along = along + jnp.where(along > REACH, NZ - NEAR, 0)
        to = lax.rem(z + along, NZ) * YC + y * NC + lax.rem(core + lax.rem(step, NC), NC)
        return to, (to, win)

    def to_smem(source):
        return pltpu.make_async_copy(table_all.at[source], table_smem.at[source], smem_sem.at[source])

    def far_to_smem():
        return pltpu.make_async_copy(table_far, table_far_smem, smem_sem.at[NZ])

    barrier = pltpu.get_barrier_semaphore()
    for step in (1, 2, 3):
        pl.semaphore_signal(barrier, inc=1, device_id=at_x(step), device_id_type=MESH)
    for step in range(1, YC):
        pl.semaphore_signal(barrier, inc=1, device_id=at_yc(step)[1], device_id_type=MESH)
    for step in range(NC, NEAR * NC):
        pl.semaphore_signal(barrier, inc=1, device_id=at_zc(step)[1], device_id_type=MESH)

    load_spectra = pltpu.make_async_copy(spectra_hbm, spectra, local_sem.at[2])
    load_spectra.start()
    load_table = pltpu.make_async_copy(table_hbm, table_all.at[z], local_sem.at[3])
    load_table.start()
    load_pairs = pltpu.make_async_copy(pairs_hbm, pairs, local_sem.at[4])
    load_pairs.start()
    load_fine = pltpu.make_async_copy(fine_hbm, fine, local_sem.at[0])
    load_fine.start()
    own_coarse = coarse_hbm.at[:, pl.ds(pl.multiple_of(win * FINE, FINE), FINE)]
    load_coarse = pltpu.make_async_copy(own_coarse, coarse, local_sem.at[1])
    load_coarse.start()

    lane_r = lax.rem(lax.broadcasted_iota(jnp.int32, (3 * 128, 128), 0), 128) // BAND
    lane_c = lax.broadcasted_iota(jnp.int32, (3 * 128, 128), 1) // BAND
    same = jnp.where(lane_r == lane_c, 1.0, 0.0).astype(jnp.bfloat16)
    chunks = WIDTH // 128
    load_spectra.wait()

    for j in range(chunks):
        re = spectra[:, j * 128 : (j + 1) * 128]
        im = spectra[:, WIDTH + j * 128 : WIDTH + (j + 1) * 128]
        rest = jnp.sqrt(re * re + im * im)
        for term in range(3):
            rounded = rest.astype(jnp.bfloat16)
            terms[j * STATIONS : (j + 1) * STATIONS, term * 128 : (term + 1) * 128] = rounded
            rest = rest - rounded.astype(jnp.float32)
    sums[...] = jnp.dot(terms[...], same, preferred_element_type=jnp.float32)
    for j in range(chunks):
        band = sums[j * STATIONS : (j + 1) * STATIONS, :] * (1.0 / BAND) + 1e-06
        inverse = 1.0 / band
        re = spectra[:, j * 128 : (j + 1) * 128]
        im = spectra[:, WIDTH + j * 128 : WIDTH + (j + 1) * 128]
        white32[pl.ds(j, STATIONS, stride=2 * chunks), :] = re * inverse
        white32[pl.ds(chunks + j, STATIONS, stride=2 * chunks), :] = im * inverse

    @pl.loop(0, STATIONS)
    def _(s):
        for step in range(NX):
            quarter = lax.rem(win + step, NX)
            base = s * 2 * chunks + quarter * ROWS
            re = white32[pl.ds(pl.multiple_of(base, ROWS), ROWS), :]
            im = white32[pl.ds(pl.multiple_of(base + chunks, ROWS), ROWS), :]
            slab = jnp.concatenate([re, im], axis=0).astype(jnp.bfloat16)
            if step == 0:
                held[0, z, s] = slab
            else:
                quarters[step - 1, s] = slab

    load_table.wait()
    to_smem(z).start()
    load_pairs.wait()
    pl.semaphore_wait(barrier, 3 + YC - 1 + NEAR * NC - NC)

    def x_copy(step):
        place = SHIFT.index((NX - step) % NX)
        return pltpu.make_async_remote_copy(
            src_ref=quarters.at[step - 1], dst_ref=held.at[place, z],
            send_sem=x_send.at[place - 1], recv_sem=x_recv.at[place - 1],
            device_id=at_x(step), device_id_type=MESH,
        )

    def z_copy(i, way, k):
        source = lax.rem(z - way * k + NZ, NZ)
        ref = held.at[i, source]
        if k == NZ // 2 - 1:
            ref = ref.at[pl.ds(0 if way == 1 else STATIONS // 2, STATIONS // 2)]
        side = 0 if way == 1 else 1
        return pltpu.make_async_remote_copy(
            src_ref=ref, dst_ref=ref, send_sem=z_send.at[i, side, k], recv_sem=z_recv.at[i, side, k],
            device_id=at_z(way), device_id_type=MESH,
        )

    def z_wait(i, way, k):
        source = lax.rem(z - way * k + NZ, NZ)
        ref = held.at[i, source]
        if k == NZ // 2:
            ref = ref.at[pl.ds(0 if way == 1 else STATIONS // 2, STATIONS // 2)]
        side = 0 if way == 1 else 1
        pltpu.make_async_copy(ref, ref, z_recv.at[i, side, k - 1]).wait()

    def t_copy(way, k):
        source = lax.rem(z - way * k + NZ, NZ)
        side = 0 if way == 1 else 1
        return pltpu.make_async_remote_copy(
            src_ref=table_all.at[source], dst_ref=table_all.at[source],
            send_sem=t_send.at[side, k], recv_sem=t_recv.at[side, k],
            device_id=at_z(way), device_id_type=MESH,
        )

    def t_wait(way, k):
        source = lax.rem(z - way * k + NZ, NZ)
        side = 0 if way == 1 else 1
        pltpu.make_async_copy(table_all.at[source], table_all.at[source], t_recv.at[side, k - 1]).wait()

    def far_copy(i):
        return pltpu.make_async_remote_copy(
            src_ref=held.at[i, z], dst_ref=far.at[FAR.index(i)],
            send_sem=f_send.at[FAR.index(i)], recv_sem=f_recv.at[FAR.index(i)],
            device_id=(z * YC + across, win), device_id_type=MESH,
        )

    def far_table_copy():
        return pltpu.make_async_remote_copy(
            src_ref=table_all.at[z], dst_ref=table_far,
            send_sem=f_send.at[len(FAR)], recv_sem=f_recv.at[len(FAR)],
            device_id=(z * YC + across, win), device_id_type=MESH,
        )

    def pick(i, source, k):
        for s in range(STATIONS):
            work[s] = held[i, source, s]
        place = source * YC + yc

        skip = i in FAR and k <= REACH

        @pl.loop(0, YC - NC if skip else YC)
        def _(turn):
            step = turn
            if skip:
                step = turn + jnp.where(turn >= YC // 2, NC, 0)
            to, device = at_yc(step)
            for c in range(CAP):
                wanted = table_smem[source, c, 0, z * YC + to]
                stage[i, source, step, c] = work[wanted]

            @pl.when(step > 0)
            def _():
                pltpu.make_async_remote_copy(
                    src_ref=stage.at[i, source, step], dst_ref=landed.at[i, pl.ds(place * CAP, CAP)],
                    send_sem=y_send.at[i], recv_sem=y_recv.at[i],
                    device_id=device, device_id_type=MESH,
                ).start()

        for c in range(CAP):
            landed[i, place * CAP + c] = stage[i, source, 0, c]

    def pick_far(i):
        at = FAR.index(i)
        if [i] == FIRST_FAR:
            far_table_copy().wait_recv()
            far_to_smem().start()
            far_to_smem().wait()
        far_copy(i).wait_recv()
        for s in range(STATIONS):
            work[s] = far[at, s]
        place = z * YC + across

        @pl.loop(0, NEAR * NC)
        def _(step):
            to, device = at_zc(step)
            for c in range(CAP):
                stage_far[at, step, c] = work[table_far_smem[c, 0, to]]

            @pl.when(step > 0)
            def _():
                pltpu.make_async_remote_copy(
                    src_ref=stage_far.at[at, step], dst_ref=landed.at[i, pl.ds(place * CAP, CAP)],
                    send_sem=y_send.at[i], recv_sem=y_recv.at[i],
                    device_id=device, device_id_type=MESH,
                ).start()

        for c in range(CAP):
            landed[i, place * CAP + c] = stage_far[at, 0, c]

    def make_wave(step):
        count = QUARTER // FINE // WAVE_STEPS

        @pl.loop(step * count, (step + 1) * count)
        def _(j):
            cc = coarse[0, pl.ds(j, 1), :]
            sc = coarse[1, pl.ds(j, 1), :]
            rows = pl.ds(pl.multiple_of(j * FINE, FINE), FINE)
            later = pl.ds(pl.multiple_of(QUARTER + j * FINE, FINE), FINE)
            wave[rows, :] = (cc * fine[0] - sc * fine[1]).astype(jnp.bfloat16)
            wave[later, :] = (-(sc * fine[0] + cc * fine[1])).astype(jnp.bfloat16)

    half = NZ // 2
    for step in (1, 3, 2):
        x_copy(step).start()
    for way in (1, -1):
        z_copy(0, way, 0).start()
        t_copy(way, 0).start()
    if 0 in FAR:
        far_copy(0).start()
    if FAR:
        far_table_copy().start()

    def sent(i):
        direct = NZ * (YC - 1)
        return CAP * (direct - NEAR * NC + NEAR * NC - 1 if i in FAR else direct)

    def cross(i):
        arrived = landed.at[i, pl.ds(0, sent(i))]
        pltpu.make_async_copy(arrived, arrived, y_recv.at[i]).wait()

        @pl.loop(0, RECV // 8)
        def _(g):
            for e in range(8):
                wide[g * 8 + e] = landed[i, g * 8 + e].astype(jnp.float32)

        @pl.loop(0, SLOTS // 8)
        def _(g):
            for e in range(8):
                p = g * 8 + e
                left = wide[pairs[0, p]]
                right = wide[pairs[1, p]]
                lre, lim = left[:ROWS], left[ROWS:]
                rre, rim = right[:ROWS], right[ROWS:]
                re = lre * rre + lim * rim
                im = lre * rim - lim * rre
                first = pl.ds(pl.multiple_of(p * 2 * ROWS, ROWS), ROWS)
                second = pl.ds(pl.multiple_of(p * 2 * ROWS + ROWS, ROWS), ROWS)
                if [i] == FIRST_CROSS:
                    stack[first, :] = re
                    stack[second, :] = im
                else:
                    stack[first, :] += re
                    stack[second, :] += im

    for event in ORDER:
        kind, i = event[0], int(event[1])
        k = int(event[2]) if len(event) > 2 else 0
        if kind == "x" and i > 0:
            pltpu.make_async_copy(quarters.at[0], held.at[i, z], x_recv.at[i - 1]).wait()
            for way in (1, -1):
                z_copy(i, way, 0).start()
            if i in FAR:
                far_copy(i).start()
        elif kind == "z":
            for way in (1, -1):
                z_wait(i, way, k)
                if k < half:
                    z_copy(i, way, k).start()
            if i == 0:
                t_wait(1, k)
                to_smem(lax.rem(z - k + NZ, NZ)).start()
                if k < half:
                    t_copy(1, k).start()
                    t_wait(-1, k)
                    to_smem(lax.rem(z + k, NZ)).start()
                    if k < half - 1:
                        t_copy(-1, k).start()
        elif kind == "p":
            sources = [lax.rem(z - k + NZ, NZ)]
            if 0 < k < half:
                sources.append(lax.rem(z + k, NZ))
            for source in sources:
                if i == 0:
                    to_smem(source).wait()
                pick(i, source, k)
        elif kind == "f":
            pick_far(i)
        elif kind == "c":
            cross(i)
        elif kind == "w":
            if i == 0:
                load_fine.wait()
                load_coarse.wait()
            make_wave(i)

    for j in range(2 * ROWS):
        lhs[:, j * 128 : (j + 1) * 128] = stack[pl.ds(j, SLOTS, stride=2 * ROWS), :].astype(jnp.bfloat16)

    sides = ((0, 1), (1, NX - 1))
    part = SHARE // 2

    def h_copy(side, step, n):
        return pltpu.make_async_remote_copy(
            src_ref=half_out.at[side, n], dst_ref=half_in.at[side, n],
            send_sem=h_send.at[side, n], recv_sem=h_recv.at[side, n],
            device_id=at_x(step), device_id_type=MESH,
        )

    def r_copy(side, step, n, late):
        first = side * part if late else (1 - side) * part
        return pltpu.make_async_remote_copy(
            src_ref=parts_out.at[side, n, pl.ds(first, part)], dst_ref=parts_in.at[side, n, pl.ds(first, part)],
            send_sem=r_send.at[side, n, int(late)], recv_sem=r_recv.at[side, n, int(late)],
            device_id=at_x(step), device_id_type=MESH,
        )

    def block(n, step, first, count):
        base = lax.rem(win + step, NX) * SHARE + first
        return total[n, pl.ds(pl.multiple_of(base, count), count), :]

    steps = LAGS // LAG_STEP
    for n in range(steps):
        columns = slice(n * LAG_STEP, (n + 1) * LAG_STEP)
        total[n] = jnp.dot(lhs[...], wave[:, columns], preferred_element_type=jnp.float32)
        for side, step in sides:
            half_out[side, n] = block(n, 2, side * part, part).astype(jnp.bfloat16)
            h_copy(side, step, n).start()
    for n in range(steps):
        for side, step in sides:
            first = (1 - side) * part
            parts_out[side, n, first : first + part] = block(n, step, first, part).astype(jnp.bfloat16)
            r_copy(side, step, n, False).start()
    for n in range(steps):
        for side, step in sides:
            first = side * part
            h_copy(side, step, n).wait_recv()
            value = block(n, step, first, part) + half_in[side, n].astype(jnp.float32)
            parts_out[side, n, first : first + part] = value.astype(jnp.bfloat16)
            r_copy(side, step, n, True).start()

    live = win * SHARE + lax.broadcasted_iota(jnp.int32, (SHARE, LAG_STEP), 0) < counts[0]
    for n in range(steps):
        value = block(n, 0, 0, SHARE)
        for side, step in sides:
            for late in (False, True):
                r_copy(side, step, n, late).wait_recv()
            value = value + parts_in[side, n].astype(jnp.float32)
        value = value * (1.0 / math.sqrt(WIDTH))
        out[:, n * LAG_STEP : (n + 1) * LAG_STEP] = jnp.where(live, value, 0.0)

    for step in (1, 2, 3):
        x_copy(step).wait_send()
    for side, step in sides:
        for n in range(steps):
            h_copy(side, step, n).wait_send()
            for late in (False, True):
                r_copy(side, step, n, late).wait_send()
    for i in range(NX):
        arrived = landed.at[i, pl.ds(0, sent(i))]
        pltpu.make_async_copy(arrived, arrived, y_send.at[i]).wait()
        for way in (1, -1):
            for k in range(half):
                z_copy(i, way, k).wait_send()
    if FAR:
        far_table_copy().wait_send()
    for i in FAR:
        far_copy(i).wait_send()
    for k in range(half):
        t_copy(1, k).wait_send()
        if k < half - 1:
            t_copy(-1, k).wait_send()


def local(spectra, wanted, pairs, counts):
    table = jnp.transpose(wanted, (2, 0, 1))
    fine, coarse = tables()
    vmem = pl.BlockSpec(memory_space=pltpu.VMEM)
    smem = pl.BlockSpec(memory_space=pltpu.SMEM)
    hbm = pl.BlockSpec(memory_space=pltpu.HBM)
    half = NZ // 2
    steps = LAGS // LAG_STEP
    bf16, f32 = jnp.bfloat16, jnp.float32
    dma = pltpu.SemaphoreType.DMA
    held_in_hbm = [
        pltpu.with_memory_space_constraint(jnp.asarray(x), pltpu.HBM) for x in (spectra[0], table, pairs.T, fine, coarse)
    ]
    return pl.pallas_call(
        kernel,
        out_shape=jax.ShapeDtypeStruct((SHARE, LAGS), f32),
        in_specs=[hbm, hbm, hbm, smem, hbm, hbm],
        out_specs=vmem,
        scratch_shapes=[
            pltpu.VMEM((STATIONS, 2 * WIDTH), f32),
            pltpu.SMEM((2, SLOTS), jnp.int32),
            pltpu.VMEM((STATIONS * WIDTH // 128, 3 * 128), bf16),
            pltpu.VMEM((STATIONS * WIDTH // 128, 128), f32),
            pltpu.VMEM((STATIONS * 2 * (WIDTH // 128), 128), f32),
            pltpu.VMEM((NX - 1, STATIONS, 2 * ROWS, 128), bf16),
            pltpu.VMEM((NX, NZ, STATIONS, 2 * ROWS, 128), bf16),
            pltpu.VMEM((STATIONS, 2 * ROWS, 128), bf16),
            pltpu.VMEM((NX, NZ, YC, CAP, 2 * ROWS, 128), bf16),
            pltpu.VMEM((NX, RECV, 2 * ROWS, 128), bf16),
            pltpu.VMEM((RECV, 2 * ROWS, 128), f32),
            pltpu.VMEM((SLOTS * 2 * ROWS, 128), f32),
            pltpu.VMEM((SLOTS, 2 * QUARTER), bf16),
            pltpu.VMEM((2 * QUARTER, LAGS), bf16),
            pltpu.VMEM((steps, SLOTS, LAG_STEP), f32),
            pltpu.VMEM((2, steps, SHARE // 2, LAG_STEP), bf16),
            pltpu.VMEM((2, steps, SHARE // 2, LAG_STEP), bf16),
            pltpu.VMEM((2, steps, SHARE, LAG_STEP), bf16),
            pltpu.VMEM((2, steps, SHARE, LAG_STEP), bf16),
            pltpu.VMEM((NZ, CAP, 1, NZ * YC), jnp.int32),
            pltpu.SMEM((NZ, CAP, 1, NZ * YC), jnp.int32),
            pltpu.VMEM((2, FINE, LAGS), f32),
            pltpu.VMEM((2, QUARTER // FINE, LAGS), f32),
            pltpu.VMEM((max(len(FAR), 1), STATIONS, 2 * ROWS, 128), bf16),
            pltpu.VMEM((max(len(FAR), 1), NEAR * NC, CAP, 2 * ROWS, 128), bf16),
            pltpu.VMEM((CAP, 1, NZ * YC), jnp.int32),
            pltpu.SMEM((CAP, 1, NZ * YC), jnp.int32),
            dma((len(FAR) + 1,)), dma((len(FAR) + 1,)),
            dma((NX - 1,)), dma((NX - 1,)),
            dma((NX, 2, half)), dma((NX, 2, half)),
            dma((2, half)), dma((2, half)),
            dma((NX,)), dma((NX,)),
            dma((2, steps)), dma((2, steps)),
            dma((2, steps, 2)), dma((2, steps, 2)),
            dma((5,)), dma((NZ + 1,)),
        ],
        compiler_params=pltpu.CompilerParams(
            collective_id=0, has_side_effects=True, vmem_limit_bytes=48 << 20
        ),
        name="correlate",
    )(*held_in_hbm[:3], counts, *held_in_hbm[3:])


def solution(mesh):
    placed = (P("win", "sta", None), P("sta", None, None), P("sta", None), P("sta"))
    return jax.shard_map(
        local, mesh=mesh, in_specs=placed, out_specs=P(("sta", "win"), None), check_vma=False
    )
```

```python
import functools

import jax
import jax.numpy as jnp
import numpy as np
from jax import lax
from jax.experimental import pallas as pl
from jax.experimental.pallas import tpu as pltpu
from jax.sharding import PartitionSpec as P

BAND = 64
LAGS = 1024
NZ, NY, NC, NX = 8, 4, 2, 4
YC = NY * NC
STATIONS = 16
CAP = 3
WIDTH = 4096
QUARTER = WIDTH // NX
ROWS = QUARTER // 128
SLOTS = 256
SHARE = SLOTS // NX
RECV = NZ * YC * CAP
TERMS = 256
SHIFT = (0, 1, 3, 2)
FAR = (0, 1)
REACH = 3
NEAR = 1 + 2 * REACH
ORDER = (
    "x0", "p00", "z01", "p01", "x1", "p10", "x2", "p20", "z02", "x3", "p30",
    "p02", "z11", "p11", "z21", "p21", "z31", "p31", "z03", "z12", "p03", "z22",
    "p22", "p12", "z04", "z32", "p04", "z13", "z23", "p13", "p23", "z33", "z14",
    "f0", "z24", "z34", "p14", "p24", "p33", "p32", "f1", "p34", "c0", "c2",
    "c1", "c3",
)
FIRST_FAR = [int(event[1]) for event in ORDER if event[0] == "f"][:1]
FIRST_CROSS = [int(event[1]) for event in ORDER if event[0] == "c"][:1]
MESH = pl.DeviceIdType.MESH


def bessel(x, count):
    top = count + 160
    f = np.zeros((top + 1,) + x.shape)
    f[top - 1] = 1e-200
    for n in range(top - 1, 0, -1):
        f[n - 1] = (2 * n + 1) / x * f[n] - f[n + 1]
        f[n - 1 :] *= np.where(np.abs(f[n - 1]) > 1e100, 1e-200, 1.0)
    order = np.arange(top + 1)[:, None]
    size = np.sqrt(np.sum((2 * order + 1) * f * f, axis=0))
    first = np.sin(x) / x
    second = (first - np.cos(x)) / x
    return f[:count] * np.sign(f[0] * first + f[1] * second) / size


def expansion():
    offset = np.arange(QUARTER) - (QUARTER - 1) / 2
    reach = (LAGS - 1) / 2
    x = 2 * np.pi * offset * reach / (2 * WIDTH)
    order = np.arange(TERMS)
    j = bessel(np.abs(x), TERMS).T * np.where(x[:, None] < 0, (-1.0) ** order, 1.0)
    turn = np.array([1, 1j, -1, -1j])[order % 4]
    into = 2 * np.sqrt(order + 0.5) * turn * j * np.exp(-1j * np.pi * offset / (2 * WIDTH))[:, None]
    into = np.block([[into.real, into.imag], [-into.imag, into.real]])
    lag = np.arange(LAGS) - LAGS // 2
    t = (lag + 0.5) / reach
    legendre = np.ones((TERMS, LAGS))
    legendre[1] = t
    for n in range(1, TERMS - 1):
        legendre[n + 1] = ((2 * n + 1) * t * legendre[n] - n * legendre[n - 1]) / (n + 1)
    legendre *= np.sqrt(order + 0.5)[:, None]
    centre = 2 * QUARTER * np.arange(NX) + QUARTER - 1
    angle = (centre[:, None] * lag[None, :]) % (4 * WIDTH) * (2 * np.pi / (4 * WIDTH))
    carrier = np.stack([np.cos(angle), np.sin(angle)]) / np.sqrt(WIDTH)
    return into, legendre, carrier


def kernel(
    spectra_hbm, table_hbm, pairs_hbm, counts, into_hbm, legendre_hbm, carrier_hbm, out,
    spectra, pairs, terms, sums, white32, quarters, held, work, stage, landed, wide, stack, lhs, total, parts_out, parts_in,
    table_all, table_smem, into, legendre, carrier,
    far, stage_far, table_far, table_far_smem, f_send, f_recv,
    x_send, x_recv, z_send, z_recv, t_send, t_recv, y_send, y_recv, r_send, r_recv, local_sem, smem_sem,
):
    win = lax.axis_index("win")
    sta = lax.axis_index("sta")
    z = sta // YC
    yc = lax.rem(sta, YC)
    y = yc // NC
    core = lax.rem(yc, NC)
    across = lax.rem(y + NY // 2, NY) * NC + core

    def at_x(step):
        return (sta, lax.rem(win + step, NX))

    def at_z(step):
        return (lax.rem(z + step + NZ, NZ) * YC + yc, win)

    def at_yc(step):
        to = lax.rem(y + step // NC, NY) * NC + lax.rem(core + lax.rem(step, NC), NC)
        return to, (z * YC + to, win)

    def at_zc(step):
        along = step // NC
        along = along + jnp.where(along > REACH, NZ - NEAR, 0)
        to = lax.rem(z + along, NZ) * YC + y * NC + lax.rem(core + lax.rem(step, NC), NC)
        return to, (to, win)

    def to_smem(source):
        return pltpu.make_async_copy(table_all.at[source], table_smem.at[source], smem_sem.at[source])

    def far_to_smem():
        return pltpu.make_async_copy(table_far, table_far_smem, smem_sem.at[NZ])

    barrier = pltpu.get_barrier_semaphore()
    for step in (1, 2, 3):
        pl.semaphore_signal(barrier, inc=1, device_id=at_x(step), device_id_type=MESH)
    for step in range(1, YC):
        pl.semaphore_signal(barrier, inc=1, device_id=at_yc(step)[1], device_id_type=MESH)
    for step in range(NC, NEAR * NC):
        pl.semaphore_signal(barrier, inc=1, device_id=at_zc(step)[1], device_id_type=MESH)

    load_spectra = pltpu.make_async_copy(spectra_hbm, spectra, local_sem.at[2])
    load_spectra.start()
    load_table = pltpu.make_async_copy(table_hbm, table_all.at[z], local_sem.at[3])
    load_table.start()
    load_pairs = pltpu.make_async_copy(pairs_hbm, pairs, local_sem.at[4])
    load_pairs.start()
    loads = [
        pltpu.make_async_copy(into_hbm, into, local_sem.at[0]),
        pltpu.make_async_copy(legendre_hbm, legendre, local_sem.at[1]),
        pltpu.make_async_copy(carrier_hbm, carrier, local_sem.at[5]),
    ]
    for load in loads:
        load.start()

    lane_r = lax.rem(lax.broadcasted_iota(jnp.int32, (3 * 128, 128), 0), 128) // BAND
    lane_c = lax.broadcasted_iota(jnp.int32, (3 * 128, 128), 1) // BAND
    same = jnp.where(lane_r == lane_c, 1.0, 0.0).astype(jnp.bfloat16)
    chunks = WIDTH // 128
    load_spectra.wait()

    for j in range(chunks):
        re = spectra[:, j * 128 : (j + 1) * 128]
        im = spectra[:, WIDTH + j * 128 : WIDTH + (j + 1) * 128]
        rest = jnp.sqrt(re * re + im * im)
        for term in range(3):
            rounded = rest.astype(jnp.bfloat16)
            terms[j * STATIONS : (j + 1) * STATIONS, term * 128 : (term + 1) * 128] = rounded
            rest = rest - rounded.astype(jnp.float32)
    sums[...] = jnp.dot(terms[...], same, preferred_element_type=jnp.float32)
    for j in range(chunks):
        band = sums[j * STATIONS : (j + 1) * STATIONS, :] * (1.0 / BAND) + 1e-06
        inverse = 1.0 / band
        re = spectra[:, j * 128 : (j + 1) * 128]
        im = spectra[:, WIDTH + j * 128 : WIDTH + (j + 1) * 128]
        white32[pl.ds(j, STATIONS, stride=2 * chunks), :] = re * inverse
        white32[pl.ds(chunks + j, STATIONS, stride=2 * chunks), :] = im * inverse

    @pl.loop(0, STATIONS)
    def _(s):
        for step in range(NX):
            quarter = lax.rem(win + step, NX)
            base = s * 2 * chunks + quarter * ROWS
            re = white32[pl.ds(pl.multiple_of(base, ROWS), ROWS), :]
            im = white32[pl.ds(pl.multiple_of(base + chunks, ROWS), ROWS), :]
            slab = jnp.concatenate([re, im], axis=0).astype(jnp.bfloat16)
            if step == 0:
                held[0, z, s] = slab
            else:
                quarters[step - 1, s] = slab

    load_table.wait()
    to_smem(z).start()
    load_pairs.wait()
    pl.semaphore_wait(barrier, 3 + YC - 1 + NEAR * NC - NC)

    def x_copy(step):
        place = SHIFT.index((NX - step) % NX)
        return pltpu.make_async_remote_copy(
            src_ref=quarters.at[step - 1], dst_ref=held.at[place, z],
            send_sem=x_send.at[place - 1], recv_sem=x_recv.at[place - 1],
            device_id=at_x(step), device_id_type=MESH,
        )

    def z_copy(i, way, k):
        source = lax.rem(z - way * k + NZ, NZ)
        ref = held.at[i, source]
        if k == NZ // 2 - 1:
            ref = ref.at[pl.ds(0 if way == 1 else STATIONS // 2, STATIONS // 2)]
        side = 0 if way == 1 else 1
        return pltpu.make_async_remote_copy(
            src_ref=ref, dst_ref=ref, send_sem=z_send.at[i, side, k], recv_sem=z_recv.at[i, side, k],
            device_id=at_z(way), device_id_type=MESH,
        )

    def z_wait(i, way, k):
        source = lax.rem(z - way * k + NZ, NZ)
        ref = held.at[i, source]
        if k == NZ // 2:
            ref = ref.at[pl.ds(0 if way == 1 else STATIONS // 2, STATIONS // 2)]
        side = 0 if way == 1 else 1
        pltpu.make_async_copy(ref, ref, z_recv.at[i, side, k - 1]).wait()

    def t_copy(way, k):
        source = lax.rem(z - way * k + NZ, NZ)
        side = 0 if way == 1 else 1
        return pltpu.make_async_remote_copy(
            src_ref=table_all.at[source], dst_ref=table_all.at[source],
            send_sem=t_send.at[side, k], recv_sem=t_recv.at[side, k],
            device_id=at_z(way), device_id_type=MESH,
        )

    def t_wait(way, k):
        source = lax.rem(z - way * k + NZ, NZ)
        side = 0 if way == 1 else 1
        pltpu.make_async_copy(table_all.at[source], table_all.at[source], t_recv.at[side, k - 1]).wait()

    def far_copy(i):
        return pltpu.make_async_remote_copy(
            src_ref=held.at[i, z], dst_ref=far.at[FAR.index(i)],
            send_sem=f_send.at[FAR.index(i)], recv_sem=f_recv.at[FAR.index(i)],
            device_id=(z * YC + across, win), device_id_type=MESH,
        )

    def far_table_copy():
        return pltpu.make_async_remote_copy(
            src_ref=table_all.at[z], dst_ref=table_far,
            send_sem=f_send.at[len(FAR)], recv_sem=f_recv.at[len(FAR)],
            device_id=(z * YC + across, win), device_id_type=MESH,
        )

    def pick(i, source, k):
        for s in range(STATIONS):
            work[s] = held[i, source, s]
        place = source * YC + yc

        skip = i in FAR and k <= REACH

        @pl.loop(0, YC - NC if skip else YC)
        def _(turn):
            step = turn
            if skip:
                step = turn + jnp.where(turn >= YC // 2, NC, 0)
            to, device = at_yc(step)
            for c in range(CAP):
                wanted = table_smem[source, c, 0, z * YC + to]
                stage[i, source, step, c] = work[wanted]

            @pl.when(step > 0)
            def _():
                pltpu.make_async_remote_copy(
                    src_ref=stage.at[i, source, step], dst_ref=landed.at[i, pl.ds(place * CAP, CAP)],
                    send_sem=y_send.at[i], recv_sem=y_recv.at[i],
                    device_id=device, device_id_type=MESH,
                ).start()

        for c in range(CAP):
            landed[i, place * CAP + c] = stage[i, source, 0, c]

    def pick_far(i):
        at = FAR.index(i)
        if [i] == FIRST_FAR:
            far_table_copy().wait_recv()
            far_to_smem().start()
            far_to_smem().wait()
        far_copy(i).wait_recv()
        for s in range(STATIONS):
            work[s] = far[at, s]
        place = z * YC + across

        @pl.loop(0, NEAR * NC)
        def _(step):
            to, device = at_zc(step)
            for c in range(CAP):
                stage_far[at, step, c] = work[table_far_smem[c, 0, to]]

            @pl.when(step > 0)
            def _():
                pltpu.make_async_remote_copy(
                    src_ref=stage_far.at[at, step], dst_ref=landed.at[i, pl.ds(place * CAP, CAP)],
                    send_sem=y_send.at[i], recv_sem=y_recv.at[i],
                    device_id=device, device_id_type=MESH,
                ).start()

        for c in range(CAP):
            landed[i, place * CAP + c] = stage_far[at, 0, c]

    half = NZ // 2
    for step in (1, 3, 2):
        x_copy(step).start()
    for way in (1, -1):
        z_copy(0, way, 0).start()
        t_copy(way, 0).start()
    if 0 in FAR:
        far_copy(0).start()
    if FAR:
        far_table_copy().start()

    def sent(i):
        direct = NZ * (YC - 1)
        return CAP * (direct - NEAR * NC + NEAR * NC - 1 if i in FAR else direct)

    def cross(i):
        arrived = landed.at[i, pl.ds(0, sent(i))]
        pltpu.make_async_copy(arrived, arrived, y_recv.at[i]).wait()

        @pl.loop(0, RECV // 8)
        def _(g):
            for e in range(8):
                wide[g * 8 + e] = landed[i, g * 8 + e].astype(jnp.float32)

        @pl.loop(0, SLOTS // 8)
        def _(g):
            for e in range(8):
                p = g * 8 + e
                left = wide[pairs[0, p]]
                right = wide[pairs[1, p]]
                lre, lim = left[:ROWS], left[ROWS:]
                rre, rim = right[:ROWS], right[ROWS:]
                re = lre * rre + lim * rim
                im = lre * rim - lim * rre
                first = pl.ds(pl.multiple_of(p * 2 * ROWS, ROWS), ROWS)
                second = pl.ds(pl.multiple_of(p * 2 * ROWS + ROWS, ROWS), ROWS)
                if [i] == FIRST_CROSS:
                    stack[first, :] = re
                    stack[second, :] = im
                else:
                    stack[first, :] += re
                    stack[second, :] += im

    for event in ORDER:
        kind, i = event[0], int(event[1])
        k = int(event[2]) if len(event) > 2 else 0
        if kind == "x" and i > 0:
            pltpu.make_async_copy(quarters.at[0], held.at[i, z], x_recv.at[i - 1]).wait()
            for way in (1, -1):
                z_copy(i, way, 0).start()
            if i in FAR:
                far_copy(i).start()
        elif kind == "z":
            for way in (1, -1):
                z_wait(i, way, k)
                if k < half:
                    z_copy(i, way, k).start()
            if i == 0:
                t_wait(1, k)
                to_smem(lax.rem(z - k + NZ, NZ)).start()
                if k < half:
                    t_copy(1, k).start()
                    t_wait(-1, k)
                    to_smem(lax.rem(z + k, NZ)).start()
                    if k < half - 1:
                        t_copy(-1, k).start()
        elif kind == "p":
            sources = [lax.rem(z - k + NZ, NZ)]
            if 0 < k < half:
                sources.append(lax.rem(z + k, NZ))
            for source in sources:
                if i == 0:
                    to_smem(source).wait()
                pick(i, source, k)
        elif kind == "f":
            pick_far(i)
        elif kind == "c":
            cross(i)

    for j in range(2 * ROWS):
        lhs[:, j * 128 : (j + 1) * 128] = stack[pl.ds(j, SLOTS, stride=2 * ROWS), :].astype(jnp.bfloat16)

    def r_copy(step, n):
        rows = pl.ds(n * SHARE, SHARE)
        return pltpu.make_async_remote_copy(
            src_ref=parts_out.at[step - 1, rows], dst_ref=parts_in.at[step, rows],
            send_sem=r_send.at[step - 1, n], recv_sem=r_recv.at[step - 1, n],
            device_id=at_x(step), device_id_type=MESH,
        )

    for load in loads:
        load.wait()
    for n in range(2):
        total[...] = jnp.dot(
            lhs[...], into[:, n * TERMS : (n + 1) * TERMS], preferred_element_type=jnp.float32
        )
        for step in (2, 1, 3, 0):
            rows = pl.ds(pl.multiple_of(lax.rem(win + step, NX) * SHARE, SHARE), SHARE)
            part = total[rows, :].astype(jnp.bfloat16)
            if step == 0:
                parts_in[0, n * SHARE : (n + 1) * SHARE] = part
            else:
                parts_out[step - 1, n * SHARE : (n + 1) * SHARE] = part
                r_copy(step, n).start()

    live = win * SHARE + lax.broadcasted_iota(jnp.int32, (SHARE, LAGS), 0) < counts[0]
    value = jnp.zeros((SHARE, LAGS), jnp.float32)
    for step in (0, 1, 3, 2):
        if step > 0:
            for n in range(2):
                r_copy(step, n).wait_recv()
        waves = jnp.dot(parts_in[step], legendre[0], preferred_element_type=jnp.float32)
        waves += jnp.dot(parts_in[step], legendre[1], preferred_element_type=jnp.float32)
        quarter = lax.rem(win - step + NX, NX)
        cos = carrier[0, pl.ds(quarter, 1), :]
        sin = carrier[1, pl.ds(quarter, 1), :]
        value = value + (waves[:SHARE] * cos - waves[SHARE:] * sin)
    out[...] = jnp.where(live, value, 0.0)

    for step in (1, 2, 3):
        x_copy(step).wait_send()
        for n in range(2):
            r_copy(step, n).wait_send()
    for i in range(NX):
        arrived = landed.at[i, pl.ds(0, sent(i))]
        pltpu.make_async_copy(arrived, arrived, y_send.at[i]).wait()
        for way in (1, -1):
            for k in range(half):
                z_copy(i, way, k).wait_send()
    if FAR:
        far_table_copy().wait_send()
    for i in FAR:
        far_copy(i).wait_send()
    for k in range(half):
        t_copy(1, k).wait_send()
        if k < half - 1:
            t_copy(-1, k).wait_send()


def local(spectra, wanted, pairs, counts):
    table = jnp.transpose(wanted, (2, 0, 1))
    into, legendre, carrier = expansion()
    high = legendre.astype(jnp.bfloat16)
    low = (legendre - high.astype(np.float64)).astype(jnp.bfloat16)
    constants = [into.astype(jnp.bfloat16), np.stack([high, low]), carrier.astype(np.float32)]
    vmem = pl.BlockSpec(memory_space=pltpu.VMEM)
    smem = pl.BlockSpec(memory_space=pltpu.SMEM)
    hbm = pl.BlockSpec(memory_space=pltpu.HBM)
    half = NZ // 2
    bf16, f32 = jnp.bfloat16, jnp.float32
    dma = pltpu.SemaphoreType.DMA
    held_in_hbm = [
        pltpu.with_memory_space_constraint(jnp.asarray(x), pltpu.HBM) for x in (spectra[0], table, pairs.T, *constants)
    ]
    return pl.pallas_call(
        kernel,
        out_shape=jax.ShapeDtypeStruct((SHARE, LAGS), f32),
        in_specs=[hbm, hbm, hbm, smem, hbm, hbm, hbm],
        out_specs=vmem,
        scratch_shapes=[
            pltpu.VMEM((STATIONS, 2 * WIDTH), f32),
            pltpu.SMEM((2, SLOTS), jnp.int32),
            pltpu.VMEM((STATIONS * WIDTH // 128, 3 * 128), bf16),
            pltpu.VMEM((STATIONS * WIDTH // 128, 128), f32),
            pltpu.VMEM((STATIONS * 2 * (WIDTH // 128), 128), f32),
            pltpu.VMEM((NX - 1, STATIONS, 2 * ROWS, 128), bf16),
            pltpu.VMEM((NX, NZ, STATIONS, 2 * ROWS, 128), bf16),
            pltpu.VMEM((STATIONS, 2 * ROWS, 128), bf16),
            pltpu.VMEM((NX, NZ, YC, CAP, 2 * ROWS, 128), bf16),
            pltpu.VMEM((NX, RECV, 2 * ROWS, 128), bf16),
            pltpu.VMEM((RECV, 2 * ROWS, 128), f32),
            pltpu.VMEM((SLOTS * 2 * ROWS, 128), f32),
            pltpu.VMEM((SLOTS, 2 * QUARTER), bf16),
            pltpu.VMEM((SLOTS, TERMS), f32),
            pltpu.VMEM((NX - 1, 2 * SHARE, TERMS), bf16),
            pltpu.VMEM((NX, 2 * SHARE, TERMS), bf16),
            pltpu.VMEM((NZ, CAP, 1, NZ * YC), jnp.int32),
            pltpu.SMEM((NZ, CAP, 1, NZ * YC), jnp.int32),
            pltpu.VMEM((2 * QUARTER, 2 * TERMS), bf16),
            pltpu.VMEM((2, TERMS, LAGS), bf16),
            pltpu.VMEM((2, NX, LAGS), f32),
            pltpu.VMEM((max(len(FAR), 1), STATIONS, 2 * ROWS, 128), bf16),
            pltpu.VMEM((max(len(FAR), 1), NEAR * NC, CAP, 2 * ROWS, 128), bf16),
            pltpu.VMEM((CAP, 1, NZ * YC), jnp.int32),
            pltpu.SMEM((CAP, 1, NZ * YC), jnp.int32),
            dma((len(FAR) + 1,)), dma((len(FAR) + 1,)),
            dma((NX - 1,)), dma((NX - 1,)),
            dma((NX, 2, half)), dma((NX, 2, half)),
            dma((2, half)), dma((2, half)),
            dma((NX,)), dma((NX,)),
            dma((NX - 1, 2)), dma((NX - 1, 2)),
            dma((6,)), dma((NZ + 1,)),
        ],
        compiler_params=pltpu.CompilerParams(
            collective_id=0, has_side_effects=True, vmem_limit_bytes=48 << 20
        ),
        name="correlate",
    )(*held_in_hbm[:3], counts, *held_in_hbm[3:])


def solution(mesh):
    placed = (P("win", "sta", None), P("sta", None, None), P("sta", None), P("sta"))
    return jax.shard_map(
        local, mesh=mesh, in_specs=placed, out_specs=P(("sta", "win"), None), check_vma=False
    )
```

```python
import functools

import jax
import jax.numpy as jnp
import numpy as np
from jax import lax
from jax.experimental import pallas as pl
from jax.experimental.pallas import tpu as pltpu
from jax.sharding import PartitionSpec as P

BAND = 64
LAGS = 1024
NZ, NY, NC, NX = 8, 4, 2, 4
YC = NY * NC
STATIONS = 16
CAP = 3
WIDTH = 4096
QUARTER = WIDTH // NX
ROWS = QUARTER // 128
SLOTS = 256
SHARE = SLOTS // NX
RECV = NZ * YC * CAP
TERMS = 256
SHIFT = (0, 1, 3, 2)
REACH = {0: 2, 1: 3, 2: 3}
FAR = tuple(REACH)
ORDER = (
    "x0", "p00", "z01", "x2", "p01", "x1", "x3", "p30", "z02", "p10", "p02", "p20",
    "z21", "p21", "z31", "p31", "z03", "z22", "p22", "z11", "p11", "z32", "p32", "z23",
    "z04", "p04", "z12", "p03", "f0", "z33", "p33", "z13", "z24", "f2", "p24", "p23",
    "z14", "z34", "p34", "p14", "f1", "p13", "c0", "p12", "c2", "c3", "c1",
)
FIRST_FAR = [int(event[1]) for event in ORDER if event[0] == "f"][:1]
CROSSES = [int(event[1]) for event in ORDER if event[0] == "c"]
SENDS = (2, 1, 3, 0)
MESH = pl.DeviceIdType.MESH


def bessel(x, count):
    top = count + 160
    f = np.zeros((top + 1,) + x.shape)
    f[top - 1] = 1e-200
    for n in range(top - 1, 0, -1):
        f[n - 1] = (2 * n + 1) / x * f[n] - f[n + 1]
        f[n - 1 :] *= np.where(np.abs(f[n - 1]) > 1e100, 1e-200, 1.0)
    order = np.arange(top + 1)[:, None]
    size = np.sqrt(np.sum((2 * order + 1) * f * f, axis=0))
    first = np.sin(x) / x
    second = (first - np.cos(x)) / x
    return f[:count] * np.sign(f[0] * first + f[1] * second) / size


def expansion():
    offset = np.arange(QUARTER) - (QUARTER - 1) / 2
    reach = (LAGS - 1) / 2
    x = 2 * np.pi * offset * reach / (2 * WIDTH)
    order = np.arange(TERMS)
    j = bessel(np.abs(x), TERMS).T * np.where(x[:, None] < 0, (-1.0) ** order, 1.0)
    turn = np.array([1, 1j, -1, -1j])[order % 4]
    into = 2 * np.sqrt(order + 0.5) * turn * j * np.exp(-1j * np.pi * offset / (2 * WIDTH))[:, None]
    into = np.block([[into.real, into.imag], [-into.imag, into.real]])
    lag = np.arange(LAGS) - LAGS // 2
    t = (lag + 0.5) / reach
    legendre = np.ones((TERMS, LAGS))
    legendre[1] = t
    for n in range(1, TERMS - 1):
        legendre[n + 1] = ((2 * n + 1) * t * legendre[n] - n * legendre[n - 1]) / (n + 1)
    legendre *= np.sqrt(order + 0.5)[:, None]
    centre = 2 * QUARTER * np.arange(NX) + QUARTER - 1
    angle = (centre[:, None] * lag[None, :]) % (4 * WIDTH) * (2 * np.pi / (4 * WIDTH))
    carrier = np.stack([np.cos(angle), np.sin(angle)]) / np.sqrt(WIDTH)
    return into, legendre, carrier


def kernel(
    spectra_hbm, table_hbm, pairs_hbm, counts, into_hbm, legendre_hbm, carrier_hbm, out,
    spectra, pairs, pairs_raw, pairs_here, terms, sums, white32, quarters, held, work, stage, landed_0, landed_1, landed_2, landed_3, stack_0, stack_1, lhs, total, parts_out, parts_in,
    table_all, table_smem, into, legendre, carrier,
    far, stage_far, table_far, table_far_smem, f_send, f_recv,
    x_send, x_recv, z_send, z_recv, t_send, t_recv, y_send, y_recv, r_send, r_recv, local_sem, smem_sem,
):
    landed = (landed_0, landed_1, landed_2, landed_3)
    stacks = (stack_0, stack_1)
    win = lax.axis_index("win")
    sta = lax.axis_index("sta")
    z = sta // YC
    yc = lax.rem(sta, YC)
    y = yc // NC
    core = lax.rem(yc, NC)
    across = lax.rem(y + NY // 2, NY) * NC + core

    def at_x(step):
        return (sta, lax.rem(win + step, NX))

    def at_z(step):
        return (lax.rem(z + step + NZ, NZ) * YC + yc, win)

    def at_yc(step):
        to = lax.rem(y + step // NC, NY) * NC + lax.rem(core + lax.rem(step, NC), NC)
        return to, (z * YC + to, win)

    def at_zc(step):
        place = step // NC
        along = jnp.where(lax.rem(place, 2) == 1, (place + 1) // 2, NZ - place // 2)
        to = lax.rem(z + along, NZ) * YC + y * NC + lax.rem(core + lax.rem(step, NC), NC)
        return to, (to, win)

    def to_smem(source):
        return pltpu.make_async_copy(table_all.at[source], table_smem.at[source], smem_sem.at[source])

    def far_to_smem():
        return pltpu.make_async_copy(table_far, table_far_smem, smem_sem.at[NZ])

    barrier = pltpu.get_barrier_semaphore()
    for step in (1, 2, 3):
        pl.semaphore_signal(barrier, inc=1, device_id=at_x(step), device_id_type=MESH)
    for step in range(1, YC):
        pl.semaphore_signal(barrier, inc=1, device_id=at_yc(step)[1], device_id_type=MESH)
    farthest = 1 + 2 * max(REACH.values())
    for step in range(NC, farthest * NC):
        pl.semaphore_signal(barrier, inc=1, device_id=at_zc(step)[1], device_id_type=MESH)

    load_spectra = pltpu.make_async_copy(spectra_hbm, spectra, local_sem.at[2])
    load_spectra.start()
    load_table = pltpu.make_async_copy(table_hbm, table_all.at[z], local_sem.at[3])
    load_table.start()
    load_pairs = pltpu.make_async_copy(pairs_hbm, pairs_raw, local_sem.at[4])
    pairs_to_smem = pltpu.make_async_copy(pairs_here, pairs, local_sem.at[6])
    load_pairs.start()
    loads = [
        pltpu.make_async_copy(into_hbm, into, local_sem.at[0]),
        pltpu.make_async_copy(legendre_hbm, legendre, local_sem.at[1]),
        pltpu.make_async_copy(carrier_hbm, carrier, local_sem.at[5]),
    ]
    for load in loads:
        load.start()

    lane_r = lax.rem(lax.broadcasted_iota(jnp.int32, (3 * 128, 128), 0), 128) // BAND
    lane_c = lax.broadcasted_iota(jnp.int32, (3 * 128, 128), 1) // BAND
    same = jnp.where(lane_r == lane_c, 1.0, 0.0).astype(jnp.bfloat16)
    chunks = WIDTH // 128
    load_spectra.wait()

    for j in range(chunks):
        re = spectra[:, j * 128 : (j + 1) * 128]
        im = spectra[:, WIDTH + j * 128 : WIDTH + (j + 1) * 128]
        rest = jnp.sqrt(re * re + im * im)
        for term in range(3):
            rounded = rest.astype(jnp.bfloat16)
            terms[j * STATIONS : (j + 1) * STATIONS, term * 128 : (term + 1) * 128] = rounded
            rest = rest - rounded.astype(jnp.float32)
    sums[...] = jnp.dot(terms[...], same, preferred_element_type=jnp.float32)
    for j in range(chunks):
        band = sums[j * STATIONS : (j + 1) * STATIONS, :] * (1.0 / BAND) + 1e-06
        inverse = 1.0 / band
        re = spectra[:, j * 128 : (j + 1) * 128]
        im = spectra[:, WIDTH + j * 128 : WIDTH + (j + 1) * 128]
        white32[pl.ds(j, STATIONS, stride=2 * chunks), :] = re * inverse
        white32[pl.ds(chunks + j, STATIONS, stride=2 * chunks), :] = im * inverse

    @pl.loop(0, STATIONS)
    def _(s):
        for step in range(NX):
            quarter = lax.rem(win + step, NX)
            base = s * 2 * chunks + quarter * ROWS
            re = white32[pl.ds(pl.multiple_of(base, ROWS), ROWS), :]
            im = white32[pl.ds(pl.multiple_of(base + chunks, ROWS), ROWS), :]
            slab = jnp.concatenate([re, im], axis=0).astype(jnp.bfloat16)
            if step == 0:
                held[0, z, s] = slab
            else:
                quarters[step - 1, s] = slab

    load_table.wait()
    to_smem(z).start()
    pl.semaphore_wait(barrier, 3 + YC - 1 + farthest * NC - NC)

    def x_copy(step):
        place = SHIFT.index((NX - step) % NX)
        return pltpu.make_async_remote_copy(
            src_ref=quarters.at[step - 1], dst_ref=held.at[place, z],
            send_sem=x_send.at[place - 1], recv_sem=x_recv.at[place - 1],
            device_id=at_x(step), device_id_type=MESH,
        )

    def z_copy(i, way, k):
        source = lax.rem(z - way * k + NZ, NZ)
        ref = held.at[i, source]
        if k == NZ // 2 - 1:
            ref = ref.at[pl.ds(0 if way == 1 else STATIONS // 2, STATIONS // 2)]
        side = 0 if way == 1 else 1
        return pltpu.make_async_remote_copy(
            src_ref=ref, dst_ref=ref, send_sem=z_send.at[i, side, k], recv_sem=z_recv.at[i, side, k],
            device_id=at_z(way), device_id_type=MESH,
        )

    def z_wait(i, way, k):
        source = lax.rem(z - way * k + NZ, NZ)
        ref = held.at[i, source]
        if k == NZ // 2:
            ref = ref.at[pl.ds(0 if way == 1 else STATIONS // 2, STATIONS // 2)]
        side = 0 if way == 1 else 1
        pltpu.make_async_copy(ref, ref, z_recv.at[i, side, k - 1]).wait()

    def t_copy(way, k):
        source = lax.rem(z - way * k + NZ, NZ)
        side = 0 if way == 1 else 1
        return pltpu.make_async_remote_copy(
            src_ref=table_all.at[source], dst_ref=table_all.at[source],
            send_sem=t_send.at[side, k], recv_sem=t_recv.at[side, k],
            device_id=at_z(way), device_id_type=MESH,
        )

    def t_wait(way, k):
        source = lax.rem(z - way * k + NZ, NZ)
        side = 0 if way == 1 else 1
        pltpu.make_async_copy(table_all.at[source], table_all.at[source], t_recv.at[side, k - 1]).wait()

    def far_copy(i):
        return pltpu.make_async_remote_copy(
            src_ref=held.at[i, z], dst_ref=far.at[FAR.index(i)],
            send_sem=f_send.at[FAR.index(i)], recv_sem=f_recv.at[FAR.index(i)],
            device_id=(z * YC + across, win), device_id_type=MESH,
        )

    def far_table_copy():
        return pltpu.make_async_remote_copy(
            src_ref=table_all.at[z], dst_ref=table_far,
            send_sem=f_send.at[len(FAR)], recv_sem=f_recv.at[len(FAR)],
            device_id=(z * YC + across, win), device_id_type=MESH,
        )

    half = NZ // 2

    def pick(i, k):
        sources = [lax.rem(z - k + NZ, NZ)]
        if 0 < k < half:
            sources.append(lax.rem(z + k, NZ))
        if i == 0:
            for source in sources:
                to_smem(source).wait()
        for n, source in enumerate(sources):
            for s in range(STATIONS):
                work[n, s] = held[i, source, s]
        count = CAP * len(sources)
        place = (yc * NZ + max(2 * k - 1, 0)) * CAP
        skip = i in FAR and k <= REACH[i]

        @pl.loop(0, YC - NC if skip else YC)
        def _(turn):
            step = turn
            if skip:
                step = turn + jnp.where(turn >= YC // 2, NC, 0)
            to, device = at_yc(step)
            for n, source in enumerate(sources):
                for c in range(CAP):
                    wanted = table_smem[source, c, 0, z * YC + to]
                    stage[i, k, step, n * CAP + c] = work[n, wanted]

            @pl.when(step > 0)
            def _():
                pltpu.make_async_remote_copy(
                    src_ref=stage.at[i, k, step, pl.ds(0, count)], dst_ref=landed[i].at[pl.ds(place, count)],
                    send_sem=y_send.at[i], recv_sem=y_recv.at[i],
                    device_id=device, device_id_type=MESH,
                ).start()

        for c in range(count):
            landed[i][place + c] = stage[i, k, 0, c]

    def pick_far(i):
        at = FAR.index(i)
        if [i] == FIRST_FAR:
            far_table_copy().wait_recv()
            far_to_smem().start()
            far_to_smem().wait()
        far_copy(i).wait_recv()
        for s in range(STATIONS):
            work[0, s] = far[at, s]
        place = across * NZ * CAP

        @pl.loop(0, (1 + 2 * REACH[i]) * NC)
        def _(step):
            to, device = at_zc(step)
            for c in range(CAP):
                stage_far[at, step, c] = work[0, table_far_smem[c, 0, to]]

            @pl.when(step > 0)
            def _():
                pltpu.make_async_remote_copy(
                    src_ref=stage_far.at[at, step], dst_ref=landed[i].at[pl.ds(place + step // NC * CAP, CAP)],
                    send_sem=y_send.at[i], recv_sem=y_recv.at[i],
                    device_id=device, device_id_type=MESH,
                ).start()

        for c in range(CAP):
            landed[i][place + c] = stage_far[at, 0, c]

    def move_pairs():
        load_pairs.wait()
        entry = pairs_raw[...]
        source = entry // CAP
        distance = lax.rem(source // YC - z + NZ, NZ)
        nearness = jnp.where(distance < half, 2 * distance, 2 * NZ - 1 - 2 * distance)
        pairs_here[...] = (lax.rem(source, YC) * NZ + nearness) * CAP + lax.rem(entry, CAP)
        pairs_to_smem.start()

    for step in (1, 3, 2):
        x_copy(step).start()
    for way in (1, -1):
        z_copy(0, way, 0).start()
        t_copy(way, 0).start()
    if 0 in FAR:
        far_copy(0).start()
    if FAR:
        far_table_copy().start()

    def sent(i):
        return CAP * (NZ * (YC - 1) - (1 if i in FAR else 0))

    def cross(i):
        if i == CROSSES[0]:
            pairs_to_smem.wait()
        arrived = landed[i].at[pl.ds(0, sent(i))]
        pltpu.make_async_copy(arrived, arrived, y_recv.at[i]).wait()

        source = landed[i]
        turn = CROSSES.index(i)
        before, after = stacks[(turn + 1) % 2], stacks[turn % 2]
        for b, step in enumerate(SENDS):
            base = lax.rem(win + step, NX) * SHARE

            @pl.loop(0, SHARE // 16)
            def _(g):
                for e in range(16):
                    p = base + g * 16 + e
                    left = source[pairs[0, p]].astype(jnp.float32)
                    right = source[pairs[1, p]].astype(jnp.float32)
                    lre, lim = left[:ROWS], left[ROWS:]
                    rre, rim = right[:ROWS], right[ROWS:]
                    re = lre * rre + lim * rim
                    im = lre * rim - lim * rre
                    row = (b * SHARE + g * 16 + e) * 2 * ROWS
                    first = pl.ds(pl.multiple_of(row, ROWS), ROWS)
                    second = pl.ds(pl.multiple_of(row + ROWS, ROWS), ROWS)
                    if turn > 0:
                        re += before[first, :]
                        im += before[second, :]
                    after[first, :] = re
                    after[second, :] = im

    for event in ORDER:
        kind, i = event[0], int(event[1])
        k = int(event[2]) if len(event) > 2 else 0
        if kind == "x" and i > 0:
            pltpu.make_async_copy(quarters.at[0], held.at[i, z], x_recv.at[i - 1]).wait()
            for way in (1, -1):
                z_copy(i, way, 0).start()
            if i in FAR:
                far_copy(i).start()
        elif kind == "z":
            for way in (1, -1):
                z_wait(i, way, k)
                if k < half:
                    z_copy(i, way, k).start()
            if i == 0:
                t_wait(1, k)
                to_smem(lax.rem(z - k + NZ, NZ)).start()
                if k < half:
                    t_copy(1, k).start()
                    t_wait(-1, k)
                    to_smem(lax.rem(z + k, NZ)).start()
                    if k < half - 1:
                        t_copy(-1, k).start()
        elif kind == "p":
            pick(i, k)
            if (i, k) == (0, 1):
                move_pairs()
        elif kind == "f":
            pick_far(i)
        elif kind == "c":
            cross(i)

    def r_copy(step):
        return pltpu.make_async_remote_copy(
            src_ref=parts_out.at[step - 1], dst_ref=parts_in.at[step],
            send_sem=r_send.at[step - 1], recv_sem=r_recv.at[step - 1],
            device_id=at_x(step), device_id_type=MESH,
        )

    for load in loads:
        load.wait()
    stack = stacks[(NX - 1) % 2]
    for side in range(2):
        rows = slice(side * 2 * SHARE, (side + 1) * 2 * SHARE)
        for j in range(2 * ROWS):
            strided = pl.ds(side * 2 * SHARE * 2 * ROWS + j, 2 * SHARE, stride=2 * ROWS)
            lhs[rows, j * 128 : (j + 1) * 128] = stack[strided, :].astype(jnp.bfloat16)
        for n in range(2):
            total[...] = jnp.dot(
                lhs[rows, :], into[:, n * TERMS : (n + 1) * TERMS], preferred_element_type=jnp.float32
            )
            for b in range(2):
                step = SENDS[2 * side + b]
                part = total[b * SHARE : (b + 1) * SHARE, :].astype(jnp.bfloat16)
                place = slice(n * SHARE, (n + 1) * SHARE)
                if step == 0:
                    parts_in[0, place] = part
                else:
                    parts_out[step - 1, place] = part
        for b in range(2):
            if SENDS[2 * side + b]:
                r_copy(SENDS[2 * side + b]).start()

    live = win * SHARE + lax.broadcasted_iota(jnp.int32, (SHARE, LAGS), 0) < counts[0]
    value = jnp.zeros((SHARE, LAGS), jnp.float32)
    for step in (0, 1, 3, 2):
        if step > 0:
            r_copy(step).wait_recv()
        waves = jnp.dot(parts_in[step], legendre[0], preferred_element_type=jnp.float32)
        waves += jnp.dot(parts_in[step], legendre[1], preferred_element_type=jnp.float32)
        quarter = lax.rem(win - step + NX, NX)
        cos = carrier[0, pl.ds(quarter, 1), :]
        sin = carrier[1, pl.ds(quarter, 1), :]
        value = value + (waves[:SHARE] * cos - waves[SHARE:] * sin)
    out[...] = jnp.where(live, value, 0.0)

    for step in (1, 2, 3):
        x_copy(step).wait_send()
        r_copy(step).wait_send()
    for i in range(NX):
        arrived = landed[i].at[pl.ds(0, sent(i))]
        pltpu.make_async_copy(arrived, arrived, y_send.at[i]).wait()
        for way in (1, -1):
            for k in range(half):
                z_copy(i, way, k).wait_send()
    if FAR:
        far_table_copy().wait_send()
    for i in FAR:
        far_copy(i).wait_send()
    for k in range(half):
        t_copy(1, k).wait_send()
        if k < half - 1:
            t_copy(-1, k).wait_send()


def local(spectra, wanted, pairs, counts):
    table = jnp.transpose(wanted, (2, 0, 1))
    into, legendre, carrier = expansion()
    high = legendre.astype(jnp.bfloat16)
    low = (legendre - high.astype(np.float64)).astype(jnp.bfloat16)
    constants = [into.astype(jnp.bfloat16), np.stack([high, low]), carrier.astype(np.float32)]
    vmem = pl.BlockSpec(memory_space=pltpu.VMEM)
    hbm = pl.BlockSpec(memory_space=pltpu.HBM)
    smem = pl.BlockSpec(memory_space=pltpu.SMEM)
    half = NZ // 2
    bf16, f32 = jnp.bfloat16, jnp.float32
    dma = pltpu.SemaphoreType.DMA
    held_in_hbm = [
        pltpu.with_memory_space_constraint(jnp.asarray(x), pltpu.HBM) for x in (spectra[0], table, pairs.T, *constants)
    ]
    return pl.pallas_call(
        kernel,
        out_shape=jax.ShapeDtypeStruct((SHARE, LAGS), f32),
        in_specs=[hbm] * 3 + [smem] + [hbm] * 3,
        out_specs=vmem,
        scratch_shapes=[
            pltpu.VMEM((STATIONS, 2 * WIDTH), f32),
            pltpu.SMEM((2, SLOTS), jnp.int32),
            pltpu.VMEM((2, SLOTS), jnp.int32),
            pltpu.VMEM((2, SLOTS), jnp.int32),
            pltpu.VMEM((STATIONS * WIDTH // 128, 3 * 128), bf16),
            pltpu.VMEM((STATIONS * WIDTH // 128, 128), f32),
            pltpu.VMEM((STATIONS * 2 * (WIDTH // 128), 128), f32),
            pltpu.VMEM((NX - 1, STATIONS, 2 * ROWS, 128), bf16),
            pltpu.VMEM((NX, NZ, STATIONS, 2 * ROWS, 128), bf16),
            pltpu.VMEM((2, STATIONS, 2 * ROWS, 128), bf16),
            pltpu.VMEM((NX, half + 1, YC, 2 * CAP, 2 * ROWS, 128), bf16),
            *[pltpu.VMEM((RECV, 2 * ROWS, 128), bf16)] * NX,
            *[pltpu.VMEM((SLOTS * 2 * ROWS, 128), f32)] * 2,
            pltpu.VMEM((SLOTS, 2 * QUARTER), bf16),
            pltpu.VMEM((2 * SHARE, TERMS), f32),
            pltpu.VMEM((NX - 1, 2 * SHARE, TERMS), bf16),
            pltpu.VMEM((NX, 2 * SHARE, TERMS), bf16),
            pltpu.VMEM((NZ, CAP, 1, NZ * YC), jnp.int32),
            pltpu.SMEM((NZ, CAP, 1, NZ * YC), jnp.int32),
            pltpu.VMEM((2 * QUARTER, 2 * TERMS), bf16),
            pltpu.VMEM((2, TERMS, LAGS), bf16),
            pltpu.VMEM((2, NX, LAGS), f32),
            pltpu.VMEM((len(FAR), STATIONS, 2 * ROWS, 128), bf16),
            pltpu.VMEM((len(FAR), (1 + 2 * max(REACH.values())) * NC, CAP, 2 * ROWS, 128), bf16),
            pltpu.VMEM((CAP, 1, NZ * YC), jnp.int32),
            pltpu.SMEM((CAP, 1, NZ * YC), jnp.int32),
            dma((len(FAR) + 1,)), dma((len(FAR) + 1,)),
            dma((NX - 1,)), dma((NX - 1,)),
            dma((NX, 2, half)), dma((NX, 2, half)),
            dma((2, half)), dma((2, half)),
            dma((NX,)), dma((NX,)),
            dma((NX - 1,)), dma((NX - 1,)),
            dma((7,)), dma((NZ + 1,)),
        ],
        compiler_params=pltpu.CompilerParams(
            collective_id=0, has_side_effects=True, vmem_limit_bytes=48 << 20
        ),
        name="correlate",
    )(*held_in_hbm[:3], counts, *held_in_hbm[3:])


def solution(mesh):
    placed = (P("win", "sta", None), P("sta", None, None), P("sta", None), P("sta"))
    return jax.shard_map(
        local, mesh=mesh, in_specs=placed, out_specs=P(("sta", "win"), None), check_vma=False
    )
```

```python
import functools

import jax
import jax.numpy as jnp
import numpy as np
from jax import lax
from jax.experimental import pallas as pl
from jax.experimental.pallas import tpu as pltpu
from jax.sharding import PartitionSpec as P

BAND = 64
LAGS = 1024
NZ, NY, NC, NX = 8, 4, 2, 4
YC = NY * NC
STATIONS = 16
CAP = 3
WIDTH = 4096
QUARTER = WIDTH // NX
ROWS = QUARTER // 128
SLOTS = 256
SHARE = SLOTS // NX
RECV = NZ * YC * CAP
TERMS = 256
PIECES = 4
SHIFT = (0, 1, 3, 2)
REACH = {0: 2, 1: 3, 2: 3}
FAR = tuple(REACH)
ORDER = (
    "x0", "p00", "z01", "x2", "p01", "x1", "x3", "p30", "z02", "p10", "p02", "p20",
    "z21", "p21", "z31", "p31", "z03", "z22", "p22", "z11", "p11", "z32", "p32", "z23",
    "z04", "p04", "z12", "p12", "p03", "f0", "z33", "p33", "z13", "z24", "f2", "p13",
    "p24", "p23", "z14", "z34", "p34", "p14", "f1", "c0", "c2", "c3", "c1",
)
FIRST_FAR = [int(event[1]) for event in ORDER if event[0] == "f"][:1]
CROSSES = [int(event[1]) for event in ORDER if event[0] == "c"]
SENDS = (2, 1, 3, 0)
MESH = pl.DeviceIdType.MESH


def bessel(x, count):
    top = count + 160
    f = np.zeros((top + 1,) + x.shape)
    f[top - 1] = 1e-200
    for n in range(top - 1, 0, -1):
        f[n - 1] = (2 * n + 1) / x * f[n] - f[n + 1]
        f[n - 1 :] *= np.where(np.abs(f[n - 1]) > 1e100, 1e-200, 1.0)
    order = np.arange(top + 1)[:, None]
    size = np.sqrt(np.sum((2 * order + 1) * f * f, axis=0))
    first = np.sin(x) / x
    second = (first - np.cos(x)) / x
    return f[:count] * np.sign(f[0] * first + f[1] * second) / size


def expansion():
    offset = np.arange(QUARTER) - (QUARTER - 1) / 2
    reach = (LAGS - 1) / 2
    x = 2 * np.pi * offset * reach / (2 * WIDTH)
    order = np.arange(TERMS)
    j = bessel(np.abs(x), TERMS).T * np.where(x[:, None] < 0, (-1.0) ** order, 1.0)
    turn = np.array([1, 1j, -1, -1j])[order % 4]
    into = 2 * np.sqrt(order + 0.5) * turn * j * np.exp(-1j * np.pi * offset / (2 * WIDTH))[:, None]
    into = np.block([[into.real, into.imag], [-into.imag, into.real]])
    lag = np.arange(LAGS) - LAGS // 2
    t = (lag + 0.5) / reach
    legendre = np.ones((TERMS, LAGS))
    legendre[1] = t
    for n in range(1, TERMS - 1):
        legendre[n + 1] = ((2 * n + 1) * t * legendre[n] - n * legendre[n - 1]) / (n + 1)
    legendre *= np.sqrt(order + 0.5)[:, None]
    centre = 2 * QUARTER * np.arange(NX) + QUARTER - 1
    angle = (centre[:, None] * lag[None, :]) % (4 * WIDTH) * (2 * np.pi / (4 * WIDTH))
    carrier = np.stack([np.cos(angle), np.sin(angle)]) / np.sqrt(WIDTH)
    return into, legendre, carrier


def kernel(
    spectra_hbm, table_hbm, pairs_hbm, counts, into_hbm, legendre_hbm, carrier_hbm, out,
    spectra, pairs, pairs_raw, pairs_here, terms, sums, white32, quarters, held, work, stage, landed_0, landed_1, landed_2, landed_3, stack_0, stack_1, lhs, total, parts_out, parts_in,
    table_all, table_smem, into, legendre, carrier,
    far, stage_far, table_far, table_far_smem, f_send, f_recv,
    x_send, x_recv, z_send, z_recv, t_send, t_recv, y_send, y_recv, r_send, r_recv, local_sem, spectra_sem, smem_sem,
):
    landed = (landed_0, landed_1, landed_2, landed_3)
    stacks = (stack_0, stack_1)
    win = lax.axis_index("win")
    sta = lax.axis_index("sta")
    z = sta // YC
    yc = lax.rem(sta, YC)
    y = yc // NC
    core = lax.rem(yc, NC)
    across = lax.rem(y + NY // 2, NY) * NC + core

    def at_x(step):
        return (sta, lax.rem(win + step, NX))

    def at_z(step):
        return (lax.rem(z + step + NZ, NZ) * YC + yc, win)

    def at_yc(step):
        to = lax.rem(y + step // NC, NY) * NC + lax.rem(core + lax.rem(step, NC), NC)
        return to, (z * YC + to, win)

    def at_zc(step):
        place = step // NC
        along = jnp.where(lax.rem(place, 2) == 1, (place + 1) // 2, NZ - place // 2)
        to = lax.rem(z + along, NZ) * YC + y * NC + lax.rem(core + lax.rem(step, NC), NC)
        return to, (to, win)

    piece = WIDTH // PIECES

    def load_spectra(n, part):
        columns = pl.ds(part * WIDTH + n * piece, piece)
        return pltpu.make_async_copy(
            spectra_hbm.at[:, columns], spectra.at[:, columns], spectra_sem.at[n, part]
        )

    for n in range(PIECES):
        for part in range(2):
            load_spectra(n, part).start()

    def to_smem(source):
        return pltpu.make_async_copy(table_all.at[source], table_smem.at[source], smem_sem.at[source])

    def far_to_smem():
        return pltpu.make_async_copy(table_far, table_far_smem, smem_sem.at[NZ])

    barrier = pltpu.get_barrier_semaphore()
    for step in (1, 2, 3):
        pl.semaphore_signal(barrier, inc=1, device_id=at_x(step), device_id_type=MESH)
    for step in range(1, YC):
        pl.semaphore_signal(barrier, inc=1, device_id=at_yc(step)[1], device_id_type=MESH)
    farthest = 1 + 2 * max(REACH.values())
    for step in range(NC, farthest * NC):
        pl.semaphore_signal(barrier, inc=1, device_id=at_zc(step)[1], device_id_type=MESH)

    load_table = pltpu.make_async_copy(table_hbm, table_all.at[z], local_sem.at[3])
    load_table.start()
    load_pairs = pltpu.make_async_copy(pairs_hbm, pairs_raw, local_sem.at[4])
    pairs_to_smem = pltpu.make_async_copy(pairs_here, pairs, local_sem.at[6])
    load_pairs.start()
    loads = [
        pltpu.make_async_copy(into_hbm, into, local_sem.at[0]),
        pltpu.make_async_copy(legendre_hbm, legendre, local_sem.at[1]),
        pltpu.make_async_copy(carrier_hbm, carrier, local_sem.at[5]),
    ]

    lane_r = lax.rem(lax.broadcasted_iota(jnp.int32, (3 * 128, 128), 0), 128) // BAND
    lane_c = lax.broadcasted_iota(jnp.int32, (3 * 128, 128), 1) // BAND
    same = jnp.where(lane_r == lane_c, 1.0, 0.0).astype(jnp.bfloat16)
    chunks = WIDTH // 128

    for j in range(chunks):
        if j % (chunks // PIECES) == 0:
            for part in range(2):
                load_spectra(j // (chunks // PIECES), part).wait()
        re = spectra[:, j * 128 : (j + 1) * 128]
        im = spectra[:, WIDTH + j * 128 : WIDTH + (j + 1) * 128]
        rest = jnp.sqrt(re * re + im * im)
        for term in range(3):
            rounded = rest.astype(jnp.bfloat16)
            terms[j * STATIONS : (j + 1) * STATIONS, term * 128 : (term + 1) * 128] = rounded
            rest = rest - rounded.astype(jnp.float32)
    sums[...] = jnp.dot(terms[...], same, preferred_element_type=jnp.float32)
    for j in range(chunks):
        band = sums[j * STATIONS : (j + 1) * STATIONS, :] * (1.0 / BAND) + 1e-06
        inverse = 1.0 / band
        re = spectra[:, j * 128 : (j + 1) * 128]
        im = spectra[:, WIDTH + j * 128 : WIDTH + (j + 1) * 128]
        white32[pl.ds(j, STATIONS, stride=2 * chunks), :] = re * inverse
        white32[pl.ds(chunks + j, STATIONS, stride=2 * chunks), :] = im * inverse

    @pl.loop(0, STATIONS)
    def _(s):
        for step in range(NX):
            quarter = lax.rem(win + step, NX)
            base = s * 2 * chunks + quarter * ROWS
            re = white32[pl.ds(pl.multiple_of(base, ROWS), ROWS), :]
            im = white32[pl.ds(pl.multiple_of(base + chunks, ROWS), ROWS), :]
            slab = jnp.concatenate([re, im], axis=0).astype(jnp.bfloat16)
            if step == 0:
                held[0, z, s] = slab
            else:
                quarters[step - 1, s] = slab

    load_table.wait()
    to_smem(z).start()
    pl.semaphore_wait(barrier, 3 + YC - 1 + farthest * NC - NC)

    def x_copy(step):
        place = SHIFT.index((NX - step) % NX)
        return pltpu.make_async_remote_copy(
            src_ref=quarters.at[step - 1], dst_ref=held.at[place, z],
            send_sem=x_send.at[place - 1], recv_sem=x_recv.at[place - 1],
            device_id=at_x(step), device_id_type=MESH,
        )

    def z_copy(i, way, k):
        source = lax.rem(z - way * k + NZ, NZ)
        ref = held.at[i, source]
        if k == NZ // 2 - 1:
            ref = ref.at[pl.ds(0 if way == 1 else STATIONS // 2, STATIONS // 2)]
        side = 0 if way == 1 else 1
        return pltpu.make_async_remote_copy(
            src_ref=ref, dst_ref=ref, send_sem=z_send.at[i, side, k], recv_sem=z_recv.at[i, side, k],
            device_id=at_z(way), device_id_type=MESH,
        )

    def z_wait(i, way, k):
        source = lax.rem(z - way * k + NZ, NZ)
        ref = held.at[i, source]
        if k == NZ // 2:
            ref = ref.at[pl.ds(0 if way == 1 else STATIONS // 2, STATIONS // 2)]
        side = 0 if way == 1 else 1
        pltpu.make_async_copy(ref, ref, z_recv.at[i, side, k - 1]).wait()

    def t_copy(way, k):
        source = lax.rem(z - way * k + NZ, NZ)
        side = 0 if way == 1 else 1
        return pltpu.make_async_remote_copy(
            src_ref=table_all.at[source], dst_ref=table_all.at[source],
            send_sem=t_send.at[side, k], recv_sem=t_recv.at[side, k],
            device_id=at_z(way), device_id_type=MESH,
        )

    def t_wait(way, k):
        source = lax.rem(z - way * k + NZ, NZ)
        side = 0 if way == 1 else 1
        pltpu.make_async_copy(table_all.at[source], table_all.at[source], t_recv.at[side, k - 1]).wait()

    def far_copy(i):
        return pltpu.make_async_remote_copy(
            src_ref=held.at[i, z], dst_ref=far.at[FAR.index(i)],
            send_sem=f_send.at[FAR.index(i)], recv_sem=f_recv.at[FAR.index(i)],
            device_id=(z * YC + across, win), device_id_type=MESH,
        )

    def far_table_copy():
        return pltpu.make_async_remote_copy(
            src_ref=table_all.at[z], dst_ref=table_far,
            send_sem=f_send.at[len(FAR)], recv_sem=f_recv.at[len(FAR)],
            device_id=(z * YC + across, win), device_id_type=MESH,
        )

    half = NZ // 2

    def pick(i, k):
        sources = [lax.rem(z - k + NZ, NZ)]
        if 0 < k < half:
            sources.append(lax.rem(z + k, NZ))
        if i == 0:
            for source in sources:
                to_smem(source).wait()
        for n, source in enumerate(sources):
            for s in range(STATIONS):
                work[n, s] = held[i, source, s]
        count = CAP * len(sources)
        place = (yc * NZ + max(2 * k - 1, 0)) * CAP
        skip = i in FAR and k <= REACH[i]

        @pl.loop(0, YC - NC if skip else YC)
        def _(turn):
            step = turn
            if skip:
                step = turn + jnp.where(turn >= YC // 2, NC, 0)
            to, device = at_yc(step)
            picked = [
                work[n, table_smem[source, c, 0, z * YC + to]]
                for n, source in enumerate(sources)
                for c in range(CAP)
            ]
            for c in range(count):
                stage[i, k, step, c] = picked[c]

            @pl.when(step > 0)
            def _():
                pltpu.make_async_remote_copy(
                    src_ref=stage.at[i, k, step, pl.ds(0, count)], dst_ref=landed[i].at[pl.ds(place, count)],
                    send_sem=y_send.at[i], recv_sem=y_recv.at[i],
                    device_id=device, device_id_type=MESH,
                ).start()

        for c in range(count):
            landed[i][place + c] = stage[i, k, 0, c]

    def pick_far(i):
        at = FAR.index(i)
        if [i] == FIRST_FAR:
            far_table_copy().wait_recv()
            far_to_smem().start()
            far_to_smem().wait()
        far_copy(i).wait_recv()
        for s in range(STATIONS):
            work[0, s] = far[at, s]
        place = across * NZ * CAP

        @pl.loop(0, (1 + 2 * REACH[i]) * NC)
        def _(step):
            to, device = at_zc(step)
            picked = [work[0, table_far_smem[c, 0, to]] for c in range(CAP)]
            for c in range(CAP):
                stage_far[at, step, c] = picked[c]

            @pl.when(step > 0)
            def _():
                pltpu.make_async_remote_copy(
                    src_ref=stage_far.at[at, step], dst_ref=landed[i].at[pl.ds(place + step // NC * CAP, CAP)],
                    send_sem=y_send.at[i], recv_sem=y_recv.at[i],
                    device_id=device, device_id_type=MESH,
                ).start()

        for c in range(CAP):
            landed[i][place + c] = stage_far[at, 0, c]

    def move_pairs():
        load_pairs.wait()
        entry = pairs_raw[...]
        source = entry // CAP
        distance = lax.rem(source // YC - z + NZ, NZ)
        nearness = jnp.where(distance < half, 2 * distance, 2 * NZ - 1 - 2 * distance)
        pairs_here[...] = (lax.rem(source, YC) * NZ + nearness) * CAP + lax.rem(entry, CAP)
        pairs_to_smem.start()

    for step in (1, 3):
        x_copy(step).start()
    for way in (1, -1):
        z_copy(0, way, 0).start()
        t_copy(way, 0).start()
    if 0 in FAR:
        far_copy(0).start()
    if FAR:
        far_table_copy().start()

    def sent(i):
        return CAP * (NZ * (YC - 1) - (1 if i in FAR else 0))

    def cross(i):
        if i == CROSSES[0]:
            pairs_to_smem.wait()
        arrived = landed[i].at[pl.ds(0, sent(i))]
        pltpu.make_async_copy(arrived, arrived, y_recv.at[i]).wait()

        source = landed[i]
        turn = CROSSES.index(i)
        before, after = stacks[(turn + 1) % 2], stacks[turn % 2]
        for b, step in enumerate(SENDS):
            base = lax.rem(win + step, NX) * SHARE

            @pl.loop(0, SHARE // 16)
            def _(g):
                for e in range(16):
                    p = base + g * 16 + e
                    left = source[pairs[0, p]].astype(jnp.float32)
                    right = source[pairs[1, p]].astype(jnp.float32)
                    lre, lim = left[:ROWS], left[ROWS:]
                    rre, rim = right[:ROWS], right[ROWS:]
                    re = lre * rre + lim * rim
                    im = lre * rim - lim * rre
                    row = (b * SHARE + g * 16 + e) * 2 * ROWS
                    first = pl.ds(pl.multiple_of(row, ROWS), ROWS)
                    second = pl.ds(pl.multiple_of(row + ROWS, ROWS), ROWS)
                    if turn > 0:
                        re += before[first, :]
                        im += before[second, :]
                    after[first, :] = re
                    after[second, :] = im

    for event in ORDER:
        kind, i = event[0], int(event[1])
        k = int(event[2]) if len(event) > 2 else 0
        if kind == "x" and i > 0:
            pltpu.make_async_copy(quarters.at[0], held.at[i, z], x_recv.at[i - 1]).wait()
            for way in (1, -1):
                z_copy(i, way, 0).start()
            if i in FAR:
                far_copy(i).start()
        elif kind == "z":
            for way in (1, -1):
                z_wait(i, way, k)
                if k < half:
                    z_copy(i, way, k).start()
            if i == 0:
                t_wait(1, k)
                to_smem(lax.rem(z - k + NZ, NZ)).start()
                if k < half:
                    t_copy(1, k).start()
                    t_wait(-1, k)
                    to_smem(lax.rem(z + k, NZ)).start()
                    if k < half - 1:
                        t_copy(-1, k).start()
        elif kind == "p":
            pick(i, k)
            if (i, k) == (0, 0):
                x_copy(2).start()
            if (i, k) == (0, 1):
                move_pairs()
                for load in loads:
                    load.start()
        elif kind == "f":
            pick_far(i)
        elif kind == "c":
            cross(i)

    def r_copy(step):
        return pltpu.make_async_remote_copy(
            src_ref=parts_out.at[step - 1], dst_ref=parts_in.at[step],
            send_sem=r_send.at[step - 1], recv_sem=r_recv.at[step - 1],
            device_id=at_x(step), device_id_type=MESH,
        )

    for load in loads:
        load.wait()
    stack = stacks[(NX - 1) % 2]
    for side in range(2):
        rows = slice(side * 2 * SHARE, (side + 1) * 2 * SHARE)
        for j in range(2 * ROWS):
            strided = pl.ds(side * 2 * SHARE * 2 * ROWS + j, 2 * SHARE, stride=2 * ROWS)
            lhs[rows, j * 128 : (j + 1) * 128] = stack[strided, :].astype(jnp.bfloat16)
        for n in range(2):
            total[...] = jnp.dot(
                lhs[rows, :], into[:, n * TERMS : (n + 1) * TERMS], preferred_element_type=jnp.float32
            )
            for b in range(2):
                step = SENDS[2 * side + b]
                part = total[b * SHARE : (b + 1) * SHARE, :].astype(jnp.bfloat16)
                place = slice(n * SHARE, (n + 1) * SHARE)
                if step == 0:
                    parts_in[0, place] = part
                else:
                    parts_out[step - 1, place] = part
        for b in range(2):
            if SENDS[2 * side + b]:
                r_copy(SENDS[2 * side + b]).start()

    for step in (1, 2, 3):
        x_copy(step).wait_send()
    for i in range(NX):
        arrived = landed[i].at[pl.ds(0, sent(i))]
        pltpu.make_async_copy(arrived, arrived, y_send.at[i]).wait()
        for way in (1, -1):
            for k in range(half):
                z_copy(i, way, k).wait_send()
    if FAR:
        far_table_copy().wait_send()
    for i in FAR:
        far_copy(i).wait_send()
    for k in range(half):
        t_copy(1, k).wait_send()
        if k < half - 1:
            t_copy(-1, k).wait_send()

    live = win * SHARE + lax.broadcasted_iota(jnp.int32, (SHARE, LAGS), 0) < counts[0]
    value = jnp.zeros((SHARE, LAGS), jnp.float32)
    for step in (0, 1, 3, 2):
        if step > 0:
            r_copy(step).wait_recv()
        waves = jnp.dot(parts_in[step], legendre[0], preferred_element_type=jnp.float32)
        waves += jnp.dot(parts_in[step], legendre[1], preferred_element_type=jnp.float32)
        quarter = lax.rem(win - step + NX, NX)
        cos = carrier[0, pl.ds(quarter, 1), :]
        sin = carrier[1, pl.ds(quarter, 1), :]
        value = value + (waves[:SHARE] * cos - waves[SHARE:] * sin)
    out[...] = jnp.where(live, value, 0.0)
    for step in (1, 2, 3):
        r_copy(step).wait_send()


def local(spectra, wanted, pairs, counts):
    table = jnp.transpose(wanted, (2, 0, 1))
    into, legendre, carrier = expansion()
    high = legendre.astype(jnp.bfloat16)
    low = (legendre - high.astype(np.float64)).astype(jnp.bfloat16)
    constants = [into.astype(jnp.bfloat16), np.stack([high, low]), carrier.astype(np.float32)]
    vmem = pl.BlockSpec(memory_space=pltpu.VMEM)
    hbm = pl.BlockSpec(memory_space=pltpu.HBM)
    smem = pl.BlockSpec(memory_space=pltpu.SMEM)
    half = NZ // 2
    bf16, f32 = jnp.bfloat16, jnp.float32
    dma = pltpu.SemaphoreType.DMA
    held_in_hbm = [
        pltpu.with_memory_space_constraint(jnp.asarray(x), pltpu.HBM) for x in (spectra[0], table, pairs.T, *constants)
    ]
    return pl.pallas_call(
        kernel,
        out_shape=jax.ShapeDtypeStruct((SHARE, LAGS), f32),
        in_specs=[hbm] * 3 + [smem] + [hbm] * 3,
        out_specs=vmem,
        scratch_shapes=[
            pltpu.VMEM((STATIONS, 2 * WIDTH), f32),
            pltpu.SMEM((2, SLOTS), jnp.int32),
            pltpu.VMEM((2, SLOTS), jnp.int32),
            pltpu.VMEM((2, SLOTS), jnp.int32),
            pltpu.VMEM((STATIONS * WIDTH // 128, 3 * 128), bf16),
            pltpu.VMEM((STATIONS * WIDTH // 128, 128), f32),
            pltpu.VMEM((STATIONS * 2 * (WIDTH // 128), 128), f32),
            pltpu.VMEM((NX - 1, STATIONS, 2 * ROWS, 128), bf16),
            pltpu.VMEM((NX, NZ, STATIONS, 2 * ROWS, 128), bf16),
            pltpu.VMEM((2, STATIONS, 2 * ROWS, 128), bf16),
            pltpu.VMEM((NX, half + 1, YC, 2 * CAP, 2 * ROWS, 128), bf16),
            *[pltpu.VMEM((RECV, 2 * ROWS, 128), bf16)] * NX,
            *[pltpu.VMEM((SLOTS * 2 * ROWS, 128), f32)] * 2,
            pltpu.VMEM((SLOTS, 2 * QUARTER), bf16),
            pltpu.VMEM((2 * SHARE, TERMS), f32),
            pltpu.VMEM((NX - 1, 2 * SHARE, TERMS), bf16),
            pltpu.VMEM((NX, 2 * SHARE, TERMS), bf16),
            pltpu.VMEM((NZ, CAP, 1, NZ * YC), jnp.int32),
            pltpu.SMEM((NZ, CAP, 1, NZ * YC), jnp.int32),
            pltpu.VMEM((2 * QUARTER, 2 * TERMS), bf16),
            pltpu.VMEM((2, TERMS, LAGS), bf16),
            pltpu.VMEM((2, NX, LAGS), f32),
            pltpu.VMEM((len(FAR), STATIONS, 2 * ROWS, 128), bf16),
            pltpu.VMEM((len(FAR), (1 + 2 * max(REACH.values())) * NC, CAP, 2 * ROWS, 128), bf16),
            pltpu.VMEM((CAP, 1, NZ * YC), jnp.int32),
            pltpu.SMEM((CAP, 1, NZ * YC), jnp.int32),
            dma((len(FAR) + 1,)), dma((len(FAR) + 1,)),
            dma((NX - 1,)), dma((NX - 1,)),
            dma((NX, 2, half)), dma((NX, 2, half)),
            dma((2, half)), dma((2, half)),
            dma((NX,)), dma((NX,)),
            dma((NX - 1,)), dma((NX - 1,)),
            dma((7,)), dma((PIECES, 2)), dma((NZ + 1,)),
        ],
        compiler_params=pltpu.CompilerParams(
            collective_id=0, has_side_effects=True, vmem_limit_bytes=48 << 20
        ),
        name="correlate",
    )(*held_in_hbm[:3], counts, *held_in_hbm[3:])


def solution(mesh):
    placed = (P("win", "sta", None), P("sta", None, None), P("sta", None), P("sta"))
    return jax.shard_map(
        local, mesh=mesh, in_specs=placed, out_specs=P(("sta", "win"), None), check_vma=False
    )
```

```python
import functools

import jax
import jax.numpy as jnp
import numpy as np
from jax import lax
from jax.experimental import pallas as pl
from jax.experimental.pallas import tpu as pltpu
from jax.sharding import PartitionSpec as P

BAND = 64
LAGS = 1024
NZ, NY, NC, NX = 8, 4, 2, 4
YC = NY * NC
STATIONS = 16
CAP = 3
WIDTH = 4096
QUARTER = WIDTH // NX
ROWS = QUARTER // 128
SLOTS = 256
SHARE = SLOTS // NX
RECV = NZ * YC * CAP
TERMS = 256
PIECES = 4
SHIFT = (0, 1, 3, 2)
REACH = {0: 2, 1: 3, 2: 3}
FAR = tuple(REACH)
ORDER = (
    "x0", "p00", "z01", "x2", "p01", "x1", "x3", "p30", "z02", "p10", "p02", "p20",
    "z21", "p21", "z31", "p31", "z03", "z22", "p22", "z11", "p11", "z32", "p32", "z23",
    "z04", "p04", "z12", "p12", "p03", "f0", "z33", "p33", "z13", "z24", "f2", "p13",
    "p24", "p23", "z14", "z34", "p34", "p14", "f1", "c0", "c2", "c3", "c1",
)
FIRST_FAR = [int(event[1]) for event in ORDER if event[0] == "f"][:1]
CROSSES = [int(event[1]) for event in ORDER if event[0] == "c"]
SENDS = (2, 1, 3, 0)
MESH = pl.DeviceIdType.MESH


def bessel(x, count):
    top = count + 160
    f = np.zeros((top + 1,) + x.shape)
    f[top - 1] = 1e-200
    for n in range(top - 1, 0, -1):
        f[n - 1] = (2 * n + 1) / x * f[n] - f[n + 1]
        f[n - 1 :] *= np.where(np.abs(f[n - 1]) > 1e100, 1e-200, 1.0)
    order = np.arange(top + 1)[:, None]
    size = np.sqrt(np.sum((2 * order + 1) * f * f, axis=0))
    first = np.sin(x) / x
    second = (first - np.cos(x)) / x
    return f[:count] * np.sign(f[0] * first + f[1] * second) / size


def expansion():
    offset = np.arange(QUARTER) - (QUARTER - 1) / 2
    reach = (LAGS - 1) / 2
    x = 2 * np.pi * offset * reach / (2 * WIDTH)
    order = np.arange(TERMS)
    j = bessel(np.abs(x), TERMS).T * np.where(x[:, None] < 0, (-1.0) ** order, 1.0)
    turn = np.array([1, 1j, -1, -1j])[order % 4]
    into = 2 * np.sqrt(order + 0.5) * turn * j * np.exp(-1j * np.pi * offset / (2 * WIDTH))[:, None]
    into = np.block([[into.real, into.imag], [-into.imag, into.real]])
    lag = np.arange(LAGS) - LAGS // 2
    t = (lag + 0.5) / reach
    legendre = np.ones((TERMS, LAGS))
    legendre[1] = t
    for n in range(1, TERMS - 1):
        legendre[n + 1] = ((2 * n + 1) * t * legendre[n] - n * legendre[n - 1]) / (n + 1)
    legendre *= np.sqrt(order + 0.5)[:, None]
    centre = 2 * QUARTER * np.arange(NX) + QUARTER - 1
    angle = (centre[:, None] * lag[None, :]) % (4 * WIDTH) * (2 * np.pi / (4 * WIDTH))
    carrier = np.stack([np.cos(angle), np.sin(angle)]) / np.sqrt(WIDTH)
    return into, legendre, carrier


def kernel(
    spectra_hbm, table_hbm, pairs_hbm, counts, into_hbm, legendre_hbm, carrier_hbm, out,
    spectra, pairs, pairs_raw, pairs_here, terms, sums, white32, quarters, held, work, stage, landed_0, landed_1, landed_2, landed_3, stack_0, stack_1, lhs, total, parts_out, parts_in,
    table_all, table_smem, into, legendre, carrier,
    far, stage_far, table_far, table_far_smem, f_send, f_recv,
    x_send, x_recv, z_send, z_recv, t_send, t_recv, y_send, y_recv, r_send, r_recv, local_sem, spectra_sem, smem_sem,
):
    landed = (landed_0, landed_1, landed_2, landed_3)
    stacks = (stack_0, stack_1)
    win = lax.axis_index("win")
    sta = lax.axis_index("sta")
    z = sta // YC
    yc = lax.rem(sta, YC)
    y = yc // NC
    core = lax.rem(yc, NC)
    across = lax.rem(y + NY // 2, NY) * NC + core

    def at_x(step):
        return (sta, lax.rem(win + step, NX))

    def at_z(step):
        return (lax.rem(z + step + NZ, NZ) * YC + yc, win)

    def at_yc(step):
        to = lax.rem(y + step // NC, NY) * NC + lax.rem(core + lax.rem(step, NC), NC)
        return to, (z * YC + to, win)

    def at_zc(step):
        place = step // NC
        along = jnp.where(lax.rem(place, 2) == 1, (place + 1) // 2, NZ - place // 2)
        to = lax.rem(z + along, NZ) * YC + y * NC + lax.rem(core + lax.rem(step, NC), NC)
        return to, (to, win)

    piece = WIDTH // PIECES

    def load_spectra(n, part):
        columns = pl.ds(part * WIDTH + n * piece, piece)
        return pltpu.make_async_copy(
            spectra_hbm.at[:, columns], spectra.at[:, columns], spectra_sem.at[n, part]
        )

    for n in range(PIECES):
        for part in range(2):
            load_spectra(n, part).start()

    def to_smem(source):
        return pltpu.make_async_copy(table_all.at[source], table_smem.at[source], smem_sem.at[source])

    def far_to_smem():
        return pltpu.make_async_copy(table_far, table_far_smem, smem_sem.at[NZ])

    barrier = pltpu.get_barrier_semaphore()
    for step in (1, 2, 3):
        pl.semaphore_signal(barrier, inc=1, device_id=at_x(step), device_id_type=MESH)
    for step in range(1, YC):
        pl.semaphore_signal(barrier, inc=1, device_id=at_yc(step)[1], device_id_type=MESH)
    farthest = 1 + 2 * max(REACH.values())
    for step in range(NC, farthest * NC):
        pl.semaphore_signal(barrier, inc=1, device_id=at_zc(step)[1], device_id_type=MESH)

    load_table = pltpu.make_async_copy(table_hbm, table_all.at[z], local_sem.at[3])
    load_table.start()
    load_pairs = pltpu.make_async_copy(pairs_hbm, pairs_raw, local_sem.at[4])
    pairs_to_smem = pltpu.make_async_copy(pairs_here, pairs, local_sem.at[6])
    load_pairs.start()
    loads = [
        pltpu.make_async_copy(into_hbm, into, local_sem.at[0]),
        pltpu.make_async_copy(legendre_hbm, legendre, local_sem.at[1]),
        pltpu.make_async_copy(carrier_hbm, carrier, local_sem.at[5]),
    ]

    lane_r = lax.rem(lax.broadcasted_iota(jnp.int32, (3 * 128, 128), 0), 128) // BAND
    lane_c = lax.broadcasted_iota(jnp.int32, (3 * 128, 128), 1) // BAND
    same = jnp.where(lane_r == lane_c, 1.0, 0.0).astype(jnp.bfloat16)
    chunks = WIDTH // 128

    for j in range(chunks):
        if j % (chunks // PIECES) == 0:
            for part in range(2):
                load_spectra(j // (chunks // PIECES), part).wait()
        re = spectra[:, j * 128 : (j + 1) * 128]
        im = spectra[:, WIDTH + j * 128 : WIDTH + (j + 1) * 128]
        rest = jnp.sqrt(re * re + im * im)
        for term in range(3):
            rounded = rest.astype(jnp.bfloat16)
            terms[j * STATIONS : (j + 1) * STATIONS, term * 128 : (term + 1) * 128] = rounded
            rest = rest - rounded.astype(jnp.float32)
    sums[...] = jnp.dot(terms[...], same, preferred_element_type=jnp.float32)
    for j in range(chunks):
        band = sums[j * STATIONS : (j + 1) * STATIONS, :] * (1.0 / BAND) + 1e-06
        inverse = 1.0 / band
        re = spectra[:, j * 128 : (j + 1) * 128]
        im = spectra[:, WIDTH + j * 128 : WIDTH + (j + 1) * 128]
        white32[pl.ds(j, STATIONS, stride=2 * chunks), :] = re * inverse
        white32[pl.ds(chunks + j, STATIONS, stride=2 * chunks), :] = im * inverse

    @pl.loop(0, STATIONS)
    def _(s):
        for step in range(NX):
            quarter = lax.rem(win + step, NX)
            base = s * 2 * chunks + quarter * ROWS
            re = white32[pl.ds(pl.multiple_of(base, ROWS), ROWS), :]
            im = white32[pl.ds(pl.multiple_of(base + chunks, ROWS), ROWS), :]
            slab = jnp.concatenate([re, im], axis=0).astype(jnp.bfloat16)
            if step == 0:
                held[0, z, s] = slab
            else:
                quarters[step - 1, s] = slab

    load_table.wait()
    to_smem(z).start()
    pl.semaphore_wait(barrier, 3 + YC - 1 + farthest * NC - NC)

    def x_copy(step):
        place = SHIFT.index((NX - step) % NX)
        return pltpu.make_async_remote_copy(
            src_ref=quarters.at[step - 1], dst_ref=held.at[place, z],
            send_sem=x_send.at[place - 1], recv_sem=x_recv.at[place - 1],
            device_id=at_x(step), device_id_type=MESH,
        )

    def z_copy(i, way, k):
        source = lax.rem(z - way * k + NZ, NZ)
        ref = held.at[i, source]
        if k == NZ // 2 - 1:
            ref = ref.at[pl.ds(0 if way == 1 else STATIONS // 2, STATIONS // 2)]
        side = 0 if way == 1 else 1
        return pltpu.make_async_remote_copy(
            src_ref=ref, dst_ref=ref, send_sem=z_send.at[i, side, k], recv_sem=z_recv.at[i, side, k],
            device_id=at_z(way), device_id_type=MESH,
        )

    def z_wait(i, way, k):
        source = lax.rem(z - way * k + NZ, NZ)
        ref = held.at[i, source]
        if k == NZ // 2:
            ref = ref.at[pl.ds(0 if way == 1 else STATIONS // 2, STATIONS // 2)]
        side = 0 if way == 1 else 1
        pltpu.make_async_copy(ref, ref, z_recv.at[i, side, k - 1]).wait()

    def t_copy(way, k):
        source = lax.rem(z - way * k + NZ, NZ)
        side = 0 if way == 1 else 1
        return pltpu.make_async_remote_copy(
            src_ref=table_all.at[source], dst_ref=table_all.at[source],
            send_sem=t_send.at[side, k], recv_sem=t_recv.at[side, k],
            device_id=at_z(way), device_id_type=MESH,
        )

    def t_wait(way, k):
        source = lax.rem(z - way * k + NZ, NZ)
        side = 0 if way == 1 else 1
        pltpu.make_async_copy(table_all.at[source], table_all.at[source], t_recv.at[side, k - 1]).wait()

    def far_copy(i):
        return pltpu.make_async_remote_copy(
            src_ref=held.at[i, z], dst_ref=far.at[FAR.index(i)],
            send_sem=f_send.at[FAR.index(i)], recv_sem=f_recv.at[FAR.index(i)],
            device_id=(z * YC + across, win), device_id_type=MESH,
        )

    def far_table_copy():
        return pltpu.make_async_remote_copy(
            src_ref=table_all.at[z], dst_ref=table_far,
            send_sem=f_send.at[len(FAR)], recv_sem=f_recv.at[len(FAR)],
            device_id=(z * YC + across, win), device_id_type=MESH,
        )

    half = NZ // 2

    def pick(i, k):
        sources = [lax.rem(z - k + NZ, NZ)]
        if 0 < k < half:
            sources.append(lax.rem(z + k, NZ))
        if i == 0:
            for source in sources:
                to_smem(source).wait()
        for n, source in enumerate(sources):
            for s in range(STATIONS):
                work[n, s] = held[i, source, s]
        count = CAP * len(sources)
        place = (yc * NZ + max(2 * k - 1, 0)) * CAP
        skip = i in FAR and k <= REACH[i]

        @pl.loop(0, YC - NC if skip else YC)
        def _(turn):
            step = lax.rem(turn + YC // 2, YC)
            if skip:
                step = turn + jnp.where(turn >= YC // 2, NC, 0)
            to, device = at_yc(step)
            picked = [
                work[n, table_smem[source, c, 0, z * YC + to]]
                for n, source in enumerate(sources)
                for c in range(CAP)
            ]
            for c in range(count):
                stage[i, k, step, c] = picked[c]

            @pl.when(step > 0)
            def _():
                pltpu.make_async_remote_copy(
                    src_ref=stage.at[i, k, step, pl.ds(0, count)], dst_ref=landed[i].at[pl.ds(place, count)],
                    send_sem=y_send.at[i], recv_sem=y_recv.at[i],
                    device_id=device, device_id_type=MESH,
                ).start()

        for c in range(count):
            landed[i][place + c] = stage[i, k, 0, c]

    def pick_far(i):
        at = FAR.index(i)
        if [i] == FIRST_FAR:
            far_table_copy().wait_recv()
            far_to_smem().start()
            far_to_smem().wait()
        far_copy(i).wait_recv()
        for s in range(STATIONS):
            work[0, s] = far[at, s]
        place = across * NZ * CAP

        count = (1 + 2 * REACH[i]) * NC

        @pl.loop(0, count)
        def _(turn):
            step = count - 1 - turn
            to, device = at_zc(step)
            picked = [work[0, table_far_smem[c, 0, to]] for c in range(CAP)]
            for c in range(CAP):
                stage_far[at, step, c] = picked[c]

            @pl.when(step > 0)
            def _():
                pltpu.make_async_remote_copy(
                    src_ref=stage_far.at[at, step], dst_ref=landed[i].at[pl.ds(place + step // NC * CAP, CAP)],
                    send_sem=y_send.at[i], recv_sem=y_recv.at[i],
                    device_id=device, device_id_type=MESH,
                ).start()

        for c in range(CAP):
            landed[i][place + c] = stage_far[at, 0, c]

    def move_pairs():
        load_pairs.wait()
        entry = pairs_raw[...]
        source = entry // CAP
        distance = lax.rem(source // YC - z + NZ, NZ)
        nearness = jnp.where(distance < half, 2 * distance, 2 * NZ - 1 - 2 * distance)
        pairs_here[...] = (lax.rem(source, YC) * NZ + nearness) * CAP + lax.rem(entry, CAP)
        pairs_to_smem.start()

    for step in (1, 3):
        x_copy(step).start()
    for way in (1, -1):
        z_copy(0, way, 0).start()
        t_copy(way, 0).start()
    if 0 in FAR:
        far_copy(0).start()
    if FAR:
        far_table_copy().start()

    def sent(i):
        return CAP * (NZ * (YC - 1) - (1 if i in FAR else 0))

    def cross(i):
        if i == CROSSES[0]:
            pairs_to_smem.wait()
        arrived = landed[i].at[pl.ds(0, sent(i))]
        pltpu.make_async_copy(arrived, arrived, y_recv.at[i]).wait()

        source = landed[i]
        turn = CROSSES.index(i)
        before, after = stacks[(turn + 1) % 2], stacks[turn % 2]
        for b, step in enumerate(SENDS):
            base = lax.rem(win + step, NX) * SHARE

            @pl.loop(0, SHARE // 16)
            def _(g):
                for e in range(16):
                    p = base + g * 16 + e
                    left = source[pairs[0, p]].astype(jnp.float32)
                    right = source[pairs[1, p]].astype(jnp.float32)
                    lre, lim = left[:ROWS], left[ROWS:]
                    rre, rim = right[:ROWS], right[ROWS:]
                    re = lre * rre + lim * rim
                    im = lre * rim - lim * rre
                    row = (b * SHARE + g * 16 + e) * 2 * ROWS
                    first = pl.ds(pl.multiple_of(row, ROWS), ROWS)
                    second = pl.ds(pl.multiple_of(row + ROWS, ROWS), ROWS)
                    if turn > 0:
                        re += before[first, :]
                        im += before[second, :]
                    after[first, :] = re
                    after[second, :] = im

    for event in ORDER:
        kind, i = event[0], int(event[1])
        k = int(event[2]) if len(event) > 2 else 0
        if kind == "x" and i > 0:
            pltpu.make_async_copy(quarters.at[0], held.at[i, z], x_recv.at[i - 1]).wait()
            for way in (1, -1):
                z_copy(i, way, 0).start()
            if i in FAR:
                far_copy(i).start()
        elif kind == "z":
            for way in (1, -1):
                z_wait(i, way, k)
                if k < half:
                    z_copy(i, way, k).start()
            if i == 0:
                t_wait(1, k)
                to_smem(lax.rem(z - k + NZ, NZ)).start()
                if k < half:
                    t_copy(1, k).start()
                    t_wait(-1, k)
                    to_smem(lax.rem(z + k, NZ)).start()
                    if k < half - 1:
                        t_copy(-1, k).start()
        elif kind == "p":
            pick(i, k)
            if (i, k) == (0, 0):
                x_copy(2).start()
            if (i, k) == (0, 1):
                move_pairs()
                for load in loads:
                    load.start()
        elif kind == "f":
            pick_far(i)
        elif kind == "c":
            cross(i)

    def r_copy(step):
        return pltpu.make_async_remote_copy(
            src_ref=parts_out.at[step - 1], dst_ref=parts_in.at[step],
            send_sem=r_send.at[step - 1], recv_sem=r_recv.at[step - 1],
            device_id=at_x(step), device_id_type=MESH,
        )

    for load in loads:
        load.wait()
    stack = stacks[(NX - 1) % 2]
    for side in range(2):
        rows = slice(side * 2 * SHARE, (side + 1) * 2 * SHARE)
        for j in range(2 * ROWS):
            strided = pl.ds(side * 2 * SHARE * 2 * ROWS + j, 2 * SHARE, stride=2 * ROWS)
            lhs[rows, j * 128 : (j + 1) * 128] = stack[strided, :].astype(jnp.bfloat16)
        for n in range(2):
            total[...] = jnp.dot(
                lhs[rows, :], into[:, n * TERMS : (n + 1) * TERMS], preferred_element_type=jnp.float32
            )
            for b in range(2):
                step = SENDS[2 * side + b]
                part = total[b * SHARE : (b + 1) * SHARE, :].astype(jnp.bfloat16)
                place = slice(n * SHARE, (n + 1) * SHARE)
                if step == 0:
                    parts_in[0, place] = part
                else:
                    parts_out[step - 1, place] = part
        for b in range(2):
            if SENDS[2 * side + b]:
                r_copy(SENDS[2 * side + b]).start()

    for step in (1, 2, 3):
        x_copy(step).wait_send()
    for i in range(NX):
        arrived = landed[i].at[pl.ds(0, sent(i))]
        pltpu.make_async_copy(arrived, arrived, y_send.at[i]).wait()
        for way in (1, -1):
            for k in range(half):
                z_copy(i, way, k).wait_send()
    if FAR:
        far_table_copy().wait_send()
    for i in FAR:
        far_copy(i).wait_send()
    for k in range(half):
        t_copy(1, k).wait_send()
        if k < half - 1:
            t_copy(-1, k).wait_send()

    live = win * SHARE + lax.broadcasted_iota(jnp.int32, (SHARE, LAGS), 0) < counts[0]
    value = jnp.zeros((SHARE, LAGS), jnp.float32)
    for step in (0, 1, 3, 2):
        if step > 0:
            r_copy(step).wait_recv()
        waves = jnp.dot(parts_in[step], legendre[0], preferred_element_type=jnp.float32)
        waves += jnp.dot(parts_in[step], legendre[1], preferred_element_type=jnp.float32)
        quarter = lax.rem(win - step + NX, NX)
        cos = carrier[0, pl.ds(quarter, 1), :]
        sin = carrier[1, pl.ds(quarter, 1), :]
        value = value + (waves[:SHARE] * cos - waves[SHARE:] * sin)
    out[...] = jnp.where(live, value, 0.0)
    for step in (1, 2, 3):
        r_copy(step).wait_send()


def local(spectra, wanted, pairs, counts):
    table = jnp.transpose(wanted, (2, 0, 1))
    into, legendre, carrier = expansion()
    high = legendre.astype(jnp.bfloat16)
    low = (legendre - high.astype(np.float64)).astype(jnp.bfloat16)
    constants = [into.astype(jnp.bfloat16), np.stack([high, low]), carrier.astype(np.float32)]
    vmem = pl.BlockSpec(memory_space=pltpu.VMEM)
    hbm = pl.BlockSpec(memory_space=pltpu.HBM)
    smem = pl.BlockSpec(memory_space=pltpu.SMEM)
    half = NZ // 2
    bf16, f32 = jnp.bfloat16, jnp.float32
    dma = pltpu.SemaphoreType.DMA
    held_in_hbm = [
        pltpu.with_memory_space_constraint(jnp.asarray(x), pltpu.HBM) for x in (spectra[0], table, pairs.T, *constants)
    ]
    return pl.pallas_call(
        kernel,
        out_shape=jax.ShapeDtypeStruct((SHARE, LAGS), f32),
        in_specs=[hbm] * 3 + [smem] + [hbm] * 3,
        out_specs=vmem,
        scratch_shapes=[
            pltpu.VMEM((STATIONS, 2 * WIDTH), f32),
            pltpu.SMEM((2, SLOTS), jnp.int32),
            pltpu.VMEM((2, SLOTS), jnp.int32),
            pltpu.VMEM((2, SLOTS), jnp.int32),
            pltpu.VMEM((STATIONS * WIDTH // 128, 3 * 128), bf16),
            pltpu.VMEM((STATIONS * WIDTH // 128, 128), f32),
            pltpu.VMEM((STATIONS * 2 * (WIDTH // 128), 128), f32),
            pltpu.VMEM((NX - 1, STATIONS, 2 * ROWS, 128), bf16),
            pltpu.VMEM((NX, NZ, STATIONS, 2 * ROWS, 128), bf16),
            pltpu.VMEM((2, STATIONS, 2 * ROWS, 128), bf16),
            pltpu.VMEM((NX, half + 1, YC, 2 * CAP, 2 * ROWS, 128), bf16),
            *[pltpu.VMEM((RECV, 2 * ROWS, 128), bf16)] * NX,
            *[pltpu.VMEM((SLOTS * 2 * ROWS, 128), f32)] * 2,
            pltpu.VMEM((SLOTS, 2 * QUARTER), bf16),
            pltpu.VMEM((2 * SHARE, TERMS), f32),
            pltpu.VMEM((NX - 1, 2 * SHARE, TERMS), bf16),
            pltpu.VMEM((NX, 2 * SHARE, TERMS), bf16),
            pltpu.VMEM((NZ, CAP, 1, NZ * YC), jnp.int32),
            pltpu.SMEM((NZ, CAP, 1, NZ * YC), jnp.int32),
            pltpu.VMEM((2 * QUARTER, 2 * TERMS), bf16),
            pltpu.VMEM((2, TERMS, LAGS), bf16),
            pltpu.VMEM((2, NX, LAGS), f32),
            pltpu.VMEM((len(FAR), STATIONS, 2 * ROWS, 128), bf16),
            pltpu.VMEM((len(FAR), (1 + 2 * max(REACH.values())) * NC, CAP, 2 * ROWS, 128), bf16),
            pltpu.VMEM((CAP, 1, NZ * YC), jnp.int32),
            pltpu.SMEM((CAP, 1, NZ * YC), jnp.int32),
            dma((len(FAR) + 1,)), dma((len(FAR) + 1,)),
            dma((NX - 1,)), dma((NX - 1,)),
            dma((NX, 2, half)), dma((NX, 2, half)),
            dma((2, half)), dma((2, half)),
            dma((NX,)), dma((NX,)),
            dma((NX - 1,)), dma((NX - 1,)),
            dma((7,)), dma((PIECES, 2)), dma((NZ + 1,)),
        ],
        compiler_params=pltpu.CompilerParams(
            collective_id=0, has_side_effects=True, vmem_limit_bytes=48 << 20
        ),
        name="correlate",
    )(*held_in_hbm[:3], counts, *held_in_hbm[3:])


def solution(mesh):
    placed = (P("win", "sta", None), P("sta", None, None), P("sta", None), P("sta"))
    return jax.shard_map(
        local, mesh=mesh, in_specs=placed, out_specs=P(("sta", "win"), None), check_vma=False
    )
```
